32 devices in a mesh: groups: 1, expert: 16 (over z, y, core), dp: 2 (over x).
Axes of the slice: x: 2, y: 2, z: 4, core: 2. Of those that a mesh axis runs over, the one named last changes fastest.
Arguments:
- tokens: bfloat16 [128, 2048], P(('groups', 'expert', 'dp')), may hold values from -6 to 6
- route_ids: int32 [128, 8], P(('groups', 'expert', 'dp')), may hold values from 0 to 15, all different within a row; in each aligned block of 4 rows (0 to 3, 4 to 7, ...) at most 4 rows name the same one
- route_weights: int32 [128, 8], P(('groups', 'expert', 'dp')), may hold values from 8192 to 65535
- w_gate: bfloat16 [16, 2048, 1024], P('expert', None, 'dp'), may hold values from -0.125 to 0.125
- w_up: bfloat16 [16, 2048, 1024], P('expert', None, 'dp'), may hold values from -0.125 to 0.125
- w_down: bfloat16 [16, 1024, 2048], P('expert', 'dp'), may hold values from -0.1875 to 0.1875
- grad_out: bfloat16 [128, 2048], P(('groups', 'expert', 'dp')), may hold values from -6 to 6
Outputs:
- layer_out: bfloat16 [128, 2048], P(('groups', 'expert', 'dp'))
- input_grad: bfloat16 [128, 2048], P(('groups', 'expert', 'dp'))
- gate_grad: bfloat16 [16, 2048, 1024], P(('groups', 'expert'), None, 'dp')
- up_grad: bfloat16 [16, 2048, 1024], P(('groups', 'expert'), None, 'dp')
- down_grad: bfloat16 [16, 1024, 2048], P(('groups', 'expert'), 'dp')
The draws below stay inside these ranges and needn't reach their ends.
Inputs may be any that keep to these rules, and one draw needn't show every extreme that they name: `route_ids`: each token names 8 different experts; the 4 tokens of one device name one expert at most 4 times, and some device's tokens reach 4.
All inputs are finite; a program needn't handle non-finite values.
Results may differ from the reference program's by a relative error of at most 0.0065.
Values may be sent and summed in bfloat16 or wider, within the bound.
No kernel may reach another device: no remote copies, remote signals or barrier semaphores. Data moves between devices by JAX's collectives and lax.ppermute only.
A program may use at most 128 MiB of HBM per device.

```python
import math
import jax
import jax.numpy as jnp
import numpy as np
from jax import lax

D = 2048
FF = 1024
TOP = 8
TOK_DEV = 4
EXPERTS = 16
CAP = 4
TOKENS = 128
N_DP = 2


def set_ends(result, key, smallest, largest):
    extent = result.shape
    index_at = [jax.random.randint(jax.random.fold_in(key, axis), (), 0, extent[axis]) for axis in range(len(extent))]
    result = result.at[tuple(index_at)].set(smallest)
    longest = extent.index(max(extent))
    index_at[longest] = (index_at[longest] + 1) % extent[longest]
    return result.at[tuple(index_at)].set(largest)


def block_levels(stream_key, dims, split, least, largest):
    gain, own = 1.0, jax.random.fold_in(stream_key, 6)
    for axis_at, blocks in split:
        heights = jnp.exp(jax.random.uniform(jax.random.fold_in(own, axis_at), (blocks,), jnp.float32, least / len(split), largest / len(split)))
        gain = gain * jnp.repeat(heights, dims[axis_at] // blocks).reshape([-1 if axis == axis_at else 1 for axis in range(len(dims))])
    return gain


def deal_out(stream_key, own, number, rows, number_of, top, most, lean):
    ranking = jax.random.permutation(stream_key, number_of)
    packed, ordinary = shares(number_of, rows * top, most, lean, True), shares(number_of, rows * top, most, lean, False)
    places = jnp.arange(number_of)

    def named(lengths, rotation):
        used = int((lengths > 0).sum())
        fixed = max(1, used // 4)
        passed = fixed + (places - fixed + rotation * (used - fixed)) % max(1, number_of - fixed)
        return jnp.zeros((number_of,), jnp.int32).at[ranking[jnp.where(places < fixed, places, passed)]].set(jnp.asarray(lengths, jnp.int32))

    lengths = jnp.where(number % 4 == 0, named(packed, number // 4), named(ordinary, number - number // 4 - 1))
    mixed = jax.random.permutation(jax.random.fold_in(own, 3), number_of)
    giver, sink = mixed[0:number_of // 2 * 2:2], mixed[1:number_of // 2 * 2:2]
    room = jnp.minimum(lengths[giver] - 1, most - lengths[sink]) // 2
    room = jnp.where((giver == ranking[0]) | (sink == ranking[0]) | (lengths[sink] == 0), 0, jnp.maximum(room, 0))
    passed = jax.random.randint(jax.random.fold_in(own, 4), (number_of // 2,), 0, 1 << 20) % (room + 1)
    lengths = lengths.at[giver].add(-passed).at[sink].add(passed)
    items = jnp.searchsorted(jnp.cumsum(lengths), jnp.arange(rows * top), side="right").astype(jnp.int32)
    listing = items.reshape(top, rows).T
    listing = listing[jax.random.permutation(jax.random.fold_in(own, 1), rows)]
    rotation = jax.random.randint(jax.random.fold_in(own, 2), (rows, 1), 0, top)
    return jnp.take_along_axis(listing, (jnp.arange(top)[None, :] + rotation) % top, axis=1)


def shares(number_of, total, reach, lean, full):
    weights = [(1 << 20) // math.isqrt(standing ** lean) + 1 for standing in range(1, number_of + 1)]
    largest = reach if full else min(reach, max(-(-total // number_of), total * weights[0] // sum(weights)))
    least = 1 if total - largest >= number_of - 1 else 0
    holding, spare = [largest] + [least] * (number_of - 1), total - largest - least * (number_of - 1)
    while spare > 0:
        free = [i for i in range(1, number_of) if holding[i] < largest] or [i for i in range(1, number_of) if holding[i] < reach]
        mass, budget = sum([weights[i] for i in free]), spare
        for i in free:
            more = min(reach - holding[i], max(1, budget * weights[i] // mass), spare)
            holding[i] = holding[i] + more
            spare = spare - more
    return np.array(holding)


def gaussian(stream_key, shape, width, bound, cuts=(), kind=jnp.bfloat16):
    values = width * jax.random.normal(stream_key, shape, jnp.float32)
    if cuts:
        values = values * block_levels(stream_key, shape, cuts, -0.22, 0.18)
    return jnp.clip(values, -bound, bound).astype(kind)


def setup_inputs(seed: int = 0, part: int = 0) -> dict:
    key_list = jax.random.split(jax.random.key(seed), 8)
    own_keys = jax.random.split(jax.random.fold_in(key_list[7], part), 8)
    tokens = gaussian(own_keys[0], (TOKENS, D), 1.0, 6.0, ((0, 32),))
    route_ids_keys = jax.random.split(jax.random.fold_in(own_keys[1], 1), TOKENS // TOK_DEV)
    route_ids_turns = jax.random.permutation(jax.random.fold_in(own_keys[1], 3), TOKENS // TOK_DEV)
    route_ids = jax.vmap(lambda own, number: deal_out(jax.random.fold_in(own_keys[1], 2), own, number, TOK_DEV, EXPERTS, TOP, CAP, 2))(route_ids_keys, route_ids_turns).reshape((TOKENS, TOP))
    route_weights = set_ends(jax.random.randint(own_keys[2], (TOKENS, TOP), 8192, 65536), jax.random.fold_in(own_keys[2], 1), 8192, 65535).astype(jnp.int32)
    w_gate = gaussian(key_list[3], (EXPERTS, D, FF), D ** -0.5, 0.125, ((0, 16), (2, 2)))
    w_up = gaussian(key_list[4], (EXPERTS, D, FF), D ** -0.5, 0.125, ((0, 16), (2, 2)))
    w_down = gaussian(key_list[5], (EXPERTS, FF, D), FF ** -0.5, 0.1875, ((0, 16), (1, 2)))
    grad_out = gaussian(own_keys[6], (TOKENS, D), 1.0, 6.0, ((0, 32),))
    return dict(tokens=tokens, route_ids=route_ids, route_weights=route_weights, w_gate=w_gate, w_up=w_up, w_down=w_down, grad_out=grad_out)


def reference(tokens, route_ids, route_weights, w_gate, w_up, w_down, grad_out):
    slice_width = FF // N_DP
    grad_wide = grad_out.astype(jnp.float32)

    def one_expert(carry, index):
        mixed, back = carry
        chosen = route_ids == index
        coef = jnp.sum(jnp.where(chosen, route_weights, 0), axis=1).astype(jnp.float32) / 65536.0
        dout = (coef[:, None] * grad_wide).astype(jnp.bfloat16)
        gate_matrix = w_gate[index]
        up_matrix = w_up[index]
        down_matrix = w_down[index]
        gate = jnp.dot(tokens, gate_matrix, preferred_element_type=jnp.float32)
        upper = jnp.dot(tokens, up_matrix, preferred_element_type=jnp.float32)
        sig = jax.nn.sigmoid(gate)
        hidden = (gate * sig * upper).astype(jnp.bfloat16)
        dact = jnp.dot(dout, down_matrix.T, preferred_element_type=jnp.float32)
        dgate = (dact * upper * sig * (1.0 + gate * (1.0 - sig))).astype(jnp.bfloat16)
        dupper = (dact * gate * sig).astype(jnp.bfloat16)
        out_sum = jnp.zeros(mixed.shape, jnp.float32)
        dx_sum = jnp.zeros(back.shape, jnp.float32)
        for part in range(N_DP):
            lower = part * slice_width
            upper_end = lower + slice_width
            piece = jnp.dot(hidden[:, lower:upper_end], down_matrix[lower:upper_end],
                            preferred_element_type=jnp.float32).astype(jnp.bfloat16)
            out_sum = out_sum + lax.optimization_barrier(piece).astype(jnp.float32)
            dpiece = (jnp.dot(dgate[:, lower:upper_end], gate_matrix[:, lower:upper_end].T,
                              preferred_element_type=jnp.float32)
                      + jnp.dot(dupper[:, lower:upper_end], up_matrix[:, lower:upper_end].T,
                                preferred_element_type=jnp.float32)).astype(jnp.bfloat16)
            dx_sum = dx_sum + lax.optimization_barrier(dpiece).astype(jnp.float32)
        mixed = mixed + coef[:, None] * out_sum
        back = back + dx_sum
        grads = (jnp.dot(tokens.T, dgate, preferred_element_type=jnp.float32).astype(jnp.bfloat16),
                 jnp.dot(tokens.T, dupper, preferred_element_type=jnp.float32).astype(jnp.bfloat16),
                 jnp.dot(hidden.T, dout, preferred_element_type=jnp.float32).astype(jnp.bfloat16))
        return (mixed, back), grads

    start = (jnp.zeros((TOKENS, D), jnp.float32), jnp.zeros((TOKENS, D), jnp.float32))
    (mixed, back), (gate_grad, up_grad, down_grad) = lax.scan(
        one_expert, start, jnp.arange(EXPERTS, dtype=jnp.int32))
    return (mixed.astype(jnp.bfloat16), back.astype(jnp.bfloat16), gate_grad, up_grad, down_grad)
```

```python
import jax
import jax.numpy as jnp
from jax import lax
from jax.experimental import pallas as pl
from jax.experimental.pallas import tpu as pltpu
from jax.sharding import PartitionSpec as P

AXES = ("expert", "dp")
CHUNK = 32
VMEM_LIMIT = 48 * 1024 * 1024
F32 = jnp.float32
BF16 = jnp.bfloat16


def vmem():
    return pl.BlockSpec(memory_space=pltpu.VMEM)


def call(body, outs, *args, flops=0, out_specs=None, **kw):
    moved = sum(a.size * a.dtype.itemsize for a in args) + sum(o.size * o.dtype.itemsize for o in outs)
    return pl.pallas_call(
        body,
        out_shape=outs,
        in_specs=[vmem() for _ in args],
        out_specs=[vmem() for _ in outs] if out_specs is None else out_specs,
        compiler_params=pltpu.CompilerParams(vmem_limit_bytes=VMEM_LIMIT),
        cost_estimate=pl.CostEstimate(flops=flops, bytes_accessed=moved, transcendentals=0),
        **kw,
    )(*args)


def shape(*dims, dtype=BF16):
    return jax.ShapeDtypeStruct(dims, dtype)


def exchange(x, mask, total):
    return lax.ppermute(x, AXES, [(i, i ^ mask) for i in range(total)])


def stages(total, core):
    bits = [1 << b for b in reversed(range(total.bit_length() - 1)) if 1 << b != core]
    pairs = [bits[i : i + 2] for i in range(0, len(bits), 2)]
    return [[p[0] * a + (p[1] * b if len(p) > 1 else 0) for a in range(2) for b in range(2 if len(p) > 1 else 1)][1:] for p in pairs]


def pack(tokens, route_ids, route_weights, grad_out, experts):
    rows, width = tokens.shape
    lanes = -(-2 * experts // 128) * 128

    def body(t_ref, i_ref, w_ref, g_ref, o_ref):
        lane = lax.broadcasted_iota(jnp.int32, (rows, lanes), 1)
        ids, weights = i_ref[...], w_ref[...]
        coded = jnp.zeros((rows, lanes), jnp.int32)
        for k in range(ids.shape[1]):
            one, w = ids[:, k : k + 1], weights[:, k : k + 1]
            coded += jnp.where(lane == one, w >> 8, 0) + jnp.where(lane == one + experts, w & 255, 0)
        both = jnp.concatenate([t_ref[...].astype(F32), g_ref[...].astype(F32)], axis=0)
        side = jnp.concatenate([coded.astype(F32), jnp.zeros((rows, lanes), F32)], axis=0)
        o_ref[0] = jnp.concatenate([both, side], axis=1).astype(BF16)

    return call(body, [shape(1, 2 * rows, width + lanes)], tokens, route_ids, route_weights, grad_out)[0]


def selector(blocks, rows, offset):
    t = lax.broadcasted_iota(jnp.int32, (blocks * rows, 2 * blocks * rows), 0)
    s = lax.broadcasted_iota(jnp.int32, (blocks * rows, 2 * blocks * rows), 1)
    return (s == (t // rows) * 2 * rows + offset + t % rows).astype(BF16)


def dot(a, b, ca=1, cb=0):
    return lax.dot_general(a, b, (((ca,), (cb,)), ((), ())), preferred_element_type=F32)


def expert_math(pieces, me, w_gate, w_up, w_down, experts, splits):
    blocks = sum(p.shape[0] for p in pieces)
    rows = pieces[0].shape[1] // 2
    width, hid = w_gate.shape
    lanes = pieces[0].shape[2] - width
    m = blocks * rows
    count = len(pieces)

    def body(*refs):
        me_ref, wg_ref, wu_ref, wd_ref = refs[count : count + 4]
        outs = refs[count + 4 :]
        parts, (t_ref, do_ref, h_ref, dg_ref, du_ref) = outs[: len(splits)], outs[len(splits) :]
        x = jnp.concatenate([r[...].reshape(-1, width + lanes) for r in refs[:count]], axis=0)
        pick_t, pick_g = selector(blocks, rows, 0), selector(blocks, rows, rows)
        token = dot(pick_t, x[:, :width]).astype(BF16)
        t_ref[...] = token
        side = dot(pick_t, x[:, width:])
        lane = lax.broadcasted_iota(jnp.int32, (m, lanes), 1)
        mine = me_ref[0]
        scale = jnp.where(lane == mine, 1.0 / 256.0, 0.0) + jnp.where(lane == mine + experts, 1.0 / 65536.0, 0.0)
        coef = jnp.sum(side * scale, axis=1, keepdims=True)
        dout = (coef * dot(pick_g, x[:, :width])).astype(BF16)
        do_ref[...] = dout
        gate = dot(token, wg_ref[...])
        upper = dot(token, wu_ref[...])
        dact = dot(dout, wd_ref[...], 1, 1)
        sig = jax.nn.sigmoid(gate)
        swish = gate * sig
        hidden = (swish * upper).astype(BF16)
        dgate = (dact * upper * sig * (1.0 + gate * (1.0 - sig))).astype(BF16)
        dupper = (dact * swish).astype(BF16)
        h_ref[...], dg_ref[...], du_ref[...] = hidden, dgate, dupper
        part = (coef * dot(hidden, wd_ref[...])).astype(BF16)
        back = (dot(dgate, wg_ref[...], 1, 1) + dot(dupper, wu_ref[...], 1, 1)).astype(BF16)
        mixed = (dot(pick_t, part, 0, 0) + dot(pick_g, back, 0, 0)).astype(BF16)
        mixed = mixed.reshape(blocks, 2 * rows, width)
        at = 0
        for ref, n in zip(parts, splits):
            ref[...] = mixed[at : at + n]
            at += n

    outs = [shape(n, 2 * rows, width) for n in splits]
    outs += [shape(m, width), shape(m, width), shape(m, hid), shape(m, hid), shape(m, hid)]
    specs = [vmem()] * count + [pl.BlockSpec(memory_space=pltpu.SMEM)] + [vmem()] * 3
    args = [*pieces, me, w_gate, w_up, w_down]
    got = pl.pallas_call(
        body,
        out_shape=outs,
        in_specs=specs,
        out_specs=[vmem() for _ in outs],
        compiler_params=pltpu.CompilerParams(vmem_limit_bytes=VMEM_LIMIT),
        cost_estimate=pl.CostEstimate(flops=12 * m * width * hid, bytes_accessed=10 << 20, transcendentals=m * hid),
    )(*args)
    return list(got[: len(splits)]), got[len(splits) :]


def grad_pair(left, rights, steps):
    m, rows = left.shape
    cols = rights[0].shape[1]
    steps = steps if rows % (128 * steps) == 0 else 1
    tile = rows // steps

    def body(l_ref, *refs):
        for r_ref, o_ref in zip(refs[: len(rights)], refs[len(rights) :]):
            o_ref[...] = dot(l_ref[...], r_ref[...], 0, 0).astype(BF16)

    return pl.pallas_call(
        body,
        grid=(steps,),
        out_shape=[shape(rows, cols) for _ in rights],
        in_specs=[pl.BlockSpec((m, tile), lambda i: (0, i))] + [pl.BlockSpec((m, cols), lambda i: (0, 0)) for _ in rights],
        out_specs=[pl.BlockSpec((tile, cols), lambda i: (i, 0)) for _ in rights],
        compiler_params=pltpu.CompilerParams(vmem_limit_bytes=VMEM_LIMIT),
        cost_estimate=pl.CostEstimate(
            flops=2 * m * rows * cols * len(rights), bytes_accessed=2 * rows * cols * len(rights), transcendentals=0
        ),
    )(left, *rights)


def add_split(terms, splits, last):
    n, rows2, width = terms[0].shape
    rows = rows2 // 2

    def body(*refs):
        total = refs[0][...].astype(F32)
        for r in refs[1 : len(terms)]:
            total += r[...].astype(F32)
        outs = refs[len(terms) :]
        if last:
            outs[0][...] = total[0, :rows].astype(BF16)
            outs[1][...] = total[0, rows:].astype(BF16)
            return
        at = 0
        for ref, k in zip(outs, splits):
            ref[...] = total[at : at + k].astype(ref.dtype)
            at += k

    if last:
        outs = [shape(rows, width), shape(rows, width)]
    else:
        outs = [shape(k, rows2, width, dtype=F32 if i == 0 else BF16) for i, k in enumerate(splits)]
    return call(body, outs, *terms)


def on_device(tokens, route_ids, route_weights, w_gate, w_up, w_down, grad_out):
    experts = w_gate.shape[0] * lax.axis_size("expert")
    core = lax.axis_size("dp")
    total = lax.axis_size("expert") * core
    plan = stages(total, core)
    me = lax.axis_index("expert").astype(jnp.int32).reshape(1)
    wg, wu, wd = w_gate[0], w_up[0], w_down[0]

    held = [pack(tokens, route_ids, route_weights, grad_out, experts)]
    for masks in plan:
        block = held[0] if len(held) == 1 else jnp.concatenate(held, axis=0)
        held = [block] + [exchange(block, mask, total) for mask in masks]
    pieces = held + [exchange(h, core, total) for h in held]

    half = total // 2
    if total <= CHUNK:
        (keep, send), kept = expert_math(pieces, me, wg, wu, wd, experts, [half, half])
    else:
        whole = jnp.concatenate(pieces, axis=0)
        sums, saved = [], []
        for at in range(0, total, CHUNK):
            (got,), rest = expert_math([whole[at : at + CHUNK]], me, wg, wu, wd, experts, [CHUNK])
            sums.append(got)
            saved.append(rest)
        got = jnp.concatenate(sums, axis=0)
        keep, send = got[:half], got[half:]
        kept = [jnp.concatenate(parts, axis=0) for parts in zip(*saved)]
    token, dout, hidden, dgate, dupper = kept

    terms = [keep, exchange(send, core, total)]
    for masks in reversed(plan):
        n = terms[0].shape[0] // (len(masks) + 1)
        mine, *others = add_split(terms, [n] * (len(masks) + 1), False)
        terms = [mine] + [exchange(o, mask, total) for o, mask in zip(others, masks)]
    mixed, back = add_split(terms, None, True)

    gate_grad, up_grad = grad_pair(token, [dgate, dupper], 4)
    (down_grad,) = grad_pair(hidden, [dout], 4)
    return mixed, back, gate_grad[None], up_grad[None], down_grad[None]


def solution(mesh):
    rows = P(("groups", "expert", "dp"), None)
    in_specs = (rows, rows, rows, P("expert", None, "dp"), P("expert", None, "dp"), P("expert", "dp", None), rows)
    hidden = P(("groups", "expert"), None, "dp")
    out_specs = (rows, rows, hidden, hidden, P(("groups", "expert"), "dp", None))
    return jax.shard_map(on_device, mesh=mesh, in_specs=in_specs, out_specs=out_specs, check_vma=False)
```

```python
import jax
import jax.numpy as jnp
from jax import lax
from jax.experimental import pallas as pl
from jax.experimental.pallas import tpu as pltpu
from jax.sharding import PartitionSpec as P

AXES = ("expert", "dp")
CHUNK = 32
ROWS = 4
VMEM_LIMIT = 16 * 1024 * 1024
F32 = jnp.float32
BF16 = jnp.bfloat16


def vmem():
    return pl.BlockSpec(memory_space=pltpu.VMEM)


def hbm():
    return pl.BlockSpec(memory_space=pltpu.HBM)


def outside(arrays):
    return [pltpu.with_memory_space_constraint(a, pltpu.HBM) for a in arrays]


def shape(*dims, dtype=BF16):
    return jax.ShapeDtypeStruct(dims, dtype)


def params():
    return pltpu.CompilerParams(vmem_limit_bytes=VMEM_LIMIT)


def cost(flops, moved):
    return pl.CostEstimate(flops=flops, bytes_accessed=moved, transcendentals=0)


def dot(a, b, ca=1, cb=0):
    return lax.dot_general(a, b, (((ca,), (cb,)), ((), ())), preferred_element_type=F32)


def exchange(x, masks, total, core):
    return lax.ppermute(x, AXES, [(i, i ^ masks[i // core % 2]) for i in range(total)])


def stages(total, core):
    bits = [1 << b for b in reversed(range(total.bit_length() - 1)) if 1 << b != core]
    plan = []
    while bits:
        a, bits = bits[0], bits[1:]
        if not bits:
            plan.append([(a, a)])
            continue
        b, bits = bits[0], bits[1:]
        if (a > core) == (b > core) and b > 2 * core:
            plan.append([(b, b), (a, a), (a + b, a + b)])
        else:
            plan.append([(b, a), (a, b), (a + b, a + b)])
    return plan


def pack(tokens, route_ids, route_weights, grad_out, experts):
    rows, width = tokens.shape
    lanes = -(-2 * experts // 128) * 128

    def body(t_in, i_in, w_in, g_in, o_ref, t_ref, i_ref, w_ref, g_ref, sems):
        pairs = ((t_in, t_ref), (i_in, i_ref), (w_in, w_ref), (g_in, g_ref))
        copies = [pltpu.make_async_copy(a, b, sems.at[k]) for k, (a, b) in enumerate(pairs)]
        for c in copies:
            c.start()
        for c in copies:
            c.wait()
        lane = lax.broadcasted_iota(jnp.int32, (rows, lanes), 1)
        ids, weights = i_ref[...], w_ref[...]
        coded = jnp.zeros((rows, lanes), jnp.int32)
        for k in range(ids.shape[1]):
            one, w = ids[:, k : k + 1], weights[:, k : k + 1]
            coded += jnp.where(lane == one, w >> 8, 0) + jnp.where(lane == one + experts, w & 255, 0)
        both = jnp.concatenate([t_ref[...].astype(F32), g_ref[...].astype(F32)], axis=0)
        side = jnp.concatenate([coded.astype(F32), jnp.zeros((rows, lanes), F32)], axis=0)
        o_ref[0] = jnp.concatenate([both, side], axis=1).astype(BF16)

    args = (tokens, route_ids, route_weights, grad_out)
    return pl.pallas_call(
        body,
        out_shape=shape(1, 2 * rows, width + lanes),
        in_specs=[hbm() for _ in args],
        out_specs=vmem(),
        scratch_shapes=[pltpu.VMEM(a.shape, a.dtype) for a in args] + [pltpu.SemaphoreType.DMA((len(args),))],
        compiler_params=params(),
        cost_estimate=cost(0, 80 << 10),
    )(*outside(args))


def fetch(arrays, after):
    def body(*refs):
        n = len(arrays)
        copies = [pltpu.make_async_copy(refs[k], refs[n + 1 + k], refs[-1].at[k]) for k in range(n)]
        for c in copies:
            c.start()
        for c in copies:
            c.wait()

    return pl.pallas_call(
        body,
        out_shape=[shape(*a.shape, dtype=a.dtype) for a in arrays],
        in_specs=[hbm() for _ in arrays] + [pl.BlockSpec(memory_space=pl.ANY)],
        out_specs=[vmem() for _ in arrays],
        scratch_shapes=[pltpu.SemaphoreType.DMA((len(arrays),))],
        compiler_params=params(),
        cost_estimate=cost(0, 12 << 20),
    )(*outside(arrays), after)


def shifted(x):
    return pltpu.roll(x, ROWS, 1)


def expert_math(pieces, me, w_gate, w_up, w_down, experts, splits):
    blocks = sum(p.shape[0] for p in pieces)
    width, hid = w_gate.shape
    lanes = pieces[0].shape[2] - width
    m = blocks * ROWS
    count = len(pieces)

    def body(*refs):
        me_ref, wg_ref, wu_ref, wd_ref = refs[count : count + 4]
        outs = refs[count + 4 :]
        parts, (t_ref, do_ref, h_ref, dg_ref, du_ref) = outs[: len(splits)], outs[len(splits) :]
        x = jnp.concatenate([r[...] for r in refs[:count]], axis=0).astype(F32)
        x = x.reshape(blocks // 2, 2, 2 * ROWS, width + lanes)
        even, odd = x[:, 0], x[:, 1]
        low = lax.broadcasted_iota(jnp.int32, (1, 2 * ROWS, 1), 1) < ROWS
        wide = jnp.where(low, even, shifted(odd)).reshape(m, width + lanes)
        token = wide[:, :width].astype(BF16)
        t_ref[...] = token
        lane = lax.broadcasted_iota(jnp.int32, (1, lanes), 1)
        mine = me_ref[0]
        scale = jnp.where(lane == mine, 1.0 / 256.0, 0.0) + jnp.where(lane == mine + experts, 1.0 / 65536.0, 0.0)
        coef = jnp.sum(wide[:, width:] * scale, axis=1, keepdims=True)
        grads = jnp.where(low, shifted(even[..., :width]), odd[..., :width]).reshape(m, width)
        dout = (coef * grads).astype(BF16)
        do_ref[...] = dout
        gate = dot(token, wg_ref[...])
        upper = dot(token, wu_ref[...])
        dact = dot(dout, wd_ref[...], 1, 1)
        sig = jax.nn.sigmoid(gate)
        swish = gate * sig
        hidden = (swish * upper).astype(BF16)
        dgate = (dact * upper * sig * (1.0 + gate * (1.0 - sig))).astype(BF16)
        dupper = (dact * swish).astype(BF16)
        h_ref[...], dg_ref[...], du_ref[...] = hidden, dgate, dupper
        part = (coef * dot(hidden, wd_ref[...])).reshape(blocks // 2, 2 * ROWS, width)
        back = (dot(dgate, wg_ref[...], 1, 1) + dot(dupper, wu_ref[...], 1, 1)).reshape(blocks // 2, 2 * ROWS, width)
        first = jnp.where(low, part, shifted(back)).astype(BF16)
        second = jnp.where(low, shifted(part), back).astype(BF16)
        mixed = jnp.stack([first, second], axis=1).reshape(blocks, 2 * ROWS, width)
        at = 0
        for ref, n in zip(parts, splits):
            ref[...] = mixed[at : at + n]
            at += n

    outs = [shape(n, 2 * ROWS, width) for n in splits]
    outs += [shape(m, width), shape(m, width), shape(m, hid), shape(m, hid), shape(m, hid)]
    got = pl.pallas_call(
        body,
        out_shape=outs,
        in_specs=[vmem()] * count + [pl.BlockSpec(memory_space=pltpu.SMEM)] + [vmem()] * 3,
        out_specs=[vmem() for _ in outs],
        compiler_params=params(),
        cost_estimate=cost(12 * m * width * hid, 10 << 20),
    )(*pieces, me, w_gate, w_up, w_down)
    return list(got[: len(splits)]), got[len(splits) :]


def weight_grads(left, rights, steps):
    m, rows = left.shape
    cols = rights[0].shape[1]
    steps = steps if rows % (128 * steps) == 0 else 1
    tile = rows // steps

    def body(l_ref, *refs):
        for r_ref, o_ref in zip(refs[: len(rights)], refs[len(rights) :]):
            o_ref[...] = dot(l_ref[...], r_ref[...], 0, 0).astype(BF16)

    return pl.pallas_call(
        body,
        grid=(steps,),
        out_shape=[shape(rows, cols) for _ in rights],
        in_specs=[pl.BlockSpec((m, tile), lambda i: (0, i))] + [pl.BlockSpec((m, cols), lambda i: (0, 0)) for _ in rights],
        out_specs=[pl.BlockSpec((tile, cols), lambda i: (i, 0)) for _ in rights],
        compiler_params=params(),
        cost_estimate=cost(2 * m * rows * cols * len(rights), 2 * rows * cols * len(rights)),
    )(left, *rights)


def add(terms, splits, after=()):
    outs = [shape(n, *terms[0].shape[1:], dtype=BF16 if i else F32) for i, n in enumerate(splits)]

    def body(*refs):
        total = refs[0][...].astype(F32)
        for r in refs[1 : len(terms)]:
            total += r[...].astype(F32)
        at = 0
        for ref, n in zip(refs[len(terms) + len(after) :], splits):
            ref[...] = total[at : at + n].astype(ref.dtype)
            at += n

    return pl.pallas_call(
        body,
        out_shape=outs,
        in_specs=[vmem() for _ in terms] + [hbm() for _ in after],
        out_specs=[vmem() for _ in outs],
        compiler_params=params(),
        cost_estimate=cost(0, 64 << 10),
    )(*terms, *outside(after))


def add_pair(one, two):
    def body(a_ref, b_ref, o_ref):
        o_ref[...] = (a_ref[...].astype(F32) + b_ref[...].astype(F32)).astype(BF16)

    return pl.pallas_call(
        body,
        out_shape=shape(*one.shape),
        in_specs=[vmem(), vmem()],
        out_specs=vmem(),
        compiler_params=params(),
        cost_estimate=cost(0, 64 << 10),
    )(one, two)


def finish(terms, after=()):
    _, _, width = terms[0].shape

    def body(*refs):
        total = refs[0][...].astype(F32)
        for r in refs[1 : len(terms)]:
            total += r[...].astype(F32)
        out_ref, back_ref = refs[len(terms) + len(after) :]
        out_ref[...] = total[0, :ROWS].astype(BF16)
        back_ref[...] = total[0, ROWS:].astype(BF16)

    return pl.pallas_call(
        body,
        out_shape=[shape(ROWS, width)] * 2,
        in_specs=[vmem() for _ in terms] + [hbm() for _ in after],
        out_specs=[vmem(), vmem()],
        compiler_params=params(),
        cost_estimate=cost(0, 64 << 10),
    )(*terms, *outside(after))


def on_device(tokens, route_ids, route_weights, w_gate, w_up, w_down, grad_out):
    experts = w_gate.shape[0] * lax.axis_size("expert")
    core = lax.axis_size("dp")
    total = lax.axis_size("expert") * core
    plan = stages(total, core)
    me = lax.axis_index("expert").astype(jnp.int32).reshape(1)
    wg, wu, wd = w_gate[0], w_up[0], w_down[0]

    held = [pack(tokens, route_ids, route_weights, grad_out, experts)]
    for masks in plan:
        block = held[0] if len(held) == 1 else jnp.concatenate(held, axis=0)
        held = [block] + [exchange(block, mask, total, core) for mask in masks]
    wg, wu, wd = fetch((wg, wu, wd), held[1])
    pieces = held + [exchange(h, (core, core), total, core) for h in held]

    ways = len(held)
    size = total // 2 // ways
    if total <= CHUNK:
        parts, kept = expert_math(pieces, me, wg, wu, wd, experts, [size] * (2 * ways))
    else:
        whole = jnp.concatenate(pieces, axis=0)
        sums, saved = [], []
        for at in range(0, total, CHUNK):
            (got,), rest = expert_math([whole[at : at + CHUNK]], me, wg, wu, wd, experts, [CHUNK])
            sums.append(got)
            saved.append(rest)
        got = jnp.concatenate(sums, axis=0)
        parts = [got[at : at + size] for at in range(0, total, size)]
        kept = [jnp.concatenate(p, axis=0) for p in zip(*saved)]
    token, dout, hidden, dgate, dupper = kept

    gate_grad, up_grad = weight_grads(token, [dgate, dupper], 2)
    (down_grad,) = weight_grads(hidden, [dout], 2)

    keep, send = parts[:ways], parts[ways:]
    arrived = [exchange(p, (core, core), total, core) for p in send]
    terms = [keep[0], arrived[0]]
    for at, mask in enumerate(plan[-1]):
        terms.append(exchange(add_pair(keep[at + 1], arrived[at + 1]), mask, total, core))
    after = (gate_grad,)
    for masks in reversed(plan[:-1]):
        mine, *others = add(terms, [terms[0].shape[0] // (len(masks) + 1)] * (len(masks) + 1), after)
        terms = [mine] + [exchange(o, mask, total, core) for o, mask in zip(others, masks)]
        after = ()
    mixed, back = finish(terms, (down_grad,))
    return mixed, back, gate_grad[None], up_grad[None], down_grad[None]


def solution(mesh):
    rows = P(("groups", "expert", "dp"), None)
    in_specs = (rows, rows, rows, P("expert", None, "dp"), P("expert", None, "dp"), P("expert", "dp", None), rows)
    hidden = P(("groups", "expert"), None, "dp")
    out_specs = (rows, rows, hidden, hidden, P(("groups", "expert"), "dp", None))
    return jax.shard_map(on_device, mesh=mesh, in_specs=in_specs, out_specs=out_specs, check_vma=False)
```

```python
import jax
import jax.numpy as jnp
from jax import lax
from jax.experimental import pallas as pl
from jax.experimental.pallas import tpu as pltpu
from jax.sharding import PartitionSpec as P

AXES = ("expert", "dp")
ROWS = 4
GROUP = 4
CHUNK = 8
VMEM_LIMIT = 16 * 1024 * 1024
F32 = jnp.float32
BF16 = jnp.bfloat16


def vmem():
    return pl.BlockSpec(memory_space=pltpu.VMEM)


def hbm():
    return pl.BlockSpec(memory_space=pltpu.HBM)


def outside(arrays):
    return [pltpu.with_memory_space_constraint(a, pltpu.HBM) for a in arrays]


def shape(*dims, dtype=BF16):
    return jax.ShapeDtypeStruct(dims, dtype)


def params():
    return pltpu.CompilerParams(vmem_limit_bytes=VMEM_LIMIT)


def cost(flops, moved):
    return pl.CostEstimate(flops=flops, bytes_accessed=moved, transcendentals=0)


def dot(a, b, ca=1, cb=0):
    return lax.dot_general(a, b, (((ca,), (cb,)), ((), ())), preferred_element_type=F32)


def exchange(x, masks, total, core):
    return lax.ppermute(x, AXES, [(i, i ^ masks[i // core % 2]) for i in range(total)])


def stages(total, core):
    bits = [1 << b for b in reversed(range(total.bit_length() - 1)) if 1 << b != core]
    plan = []
    while bits:
        a, bits = bits[0], bits[1:]
        if not bits:
            plan.append([(a, a)])
            continue
        b, bits = bits[0], bits[1:]
        if (a > core) == (b > core) and b > 2 * core:
            plan.append([(b, b), (a, a), (a + b, a + b)])
        else:
            plan.append([(b, a), (a, b), (a + b, a + b)])
    return plan


def pack(tokens, route_ids, route_weights, grad_out, experts):
    rows, width = tokens.shape
    lanes = -(-2 * experts // 128) * 128

    def body(t_in, i_in, w_in, g_in, o_ref, t_ref, i_ref, w_ref, g_ref, sems):
        pairs = ((t_in, t_ref), (i_in, i_ref), (w_in, w_ref), (g_in, g_ref))
        copies = [pltpu.make_async_copy(a, b, sems.at[k]) for k, (a, b) in enumerate(pairs)]
        for c in copies:
            c.start()
        for c in copies:
            c.wait()
        lane = lax.broadcasted_iota(jnp.int32, (rows, lanes), 1)
        ids, weights = i_ref[...], w_ref[...]
        coded = jnp.zeros((rows, lanes), jnp.int32)
        for k in range(ids.shape[1]):
            one, w = ids[:, k : k + 1], weights[:, k : k + 1]
            coded += jnp.where(lane == one, w >> 8, 0) + jnp.where(lane == one + experts, w & 255, 0)
        both = jnp.concatenate([t_ref[...].astype(F32), g_ref[...].astype(F32)], axis=0)
        side = jnp.concatenate([coded.astype(F32), jnp.zeros((rows, lanes), F32)], axis=0)
        o_ref[0] = jnp.concatenate([both, side], axis=1).astype(BF16)

    args = (tokens, route_ids, route_weights, grad_out)
    return pl.pallas_call(
        body,
        out_shape=shape(1, 2 * rows, width + lanes),
        in_specs=[hbm() for _ in args],
        out_specs=vmem(),
        scratch_shapes=[pltpu.VMEM(a.shape, a.dtype) for a in args] + [pltpu.SemaphoreType.DMA((len(args),))],
        compiler_params=params(),
        cost_estimate=cost(0, 80 << 10),
    )(*outside(args))


def fetch(arrays, after):
    def body(*refs):
        n = len(arrays)
        copies = [pltpu.make_async_copy(refs[k], refs[n + 1 + k], refs[-1].at[k]) for k in range(n)]
        for c in copies:
            c.start()
        for c in copies:
            c.wait()

    return pl.pallas_call(
        body,
        out_shape=[shape(*a.shape, dtype=a.dtype) for a in arrays],
        in_specs=[hbm() for _ in arrays] + [pl.BlockSpec(memory_space=pl.ANY)],
        out_specs=[vmem() for _ in arrays],
        scratch_shapes=[pltpu.SemaphoreType.DMA((len(arrays),))],
        compiler_params=params(),
        cost_estimate=cost(0, 12 << 20),
    )(*outside(arrays), after)


def regroup(blocks):
    _, rows, width = blocks[0].shape

    def body(*refs):
        x = [r[0].astype(F32) for r in refs[:-1]]
        low = lax.broadcasted_iota(jnp.int32, (rows, 1), 0) < ROWS
        pairs = list(zip(x[::2], x[1::2]))
        token = [jnp.where(low, a, pltpu.roll(b, ROWS, 0)) for a, b in pairs]
        grads = [jnp.where(low, pltpu.roll(a, ROWS, 0), b) for a, b in pairs]
        refs[-1][0] = jnp.concatenate(token + grads, axis=0).astype(BF16)

    return pl.pallas_call(
        body,
        out_shape=shape(1, rows * len(blocks), width),
        in_specs=[vmem() for _ in blocks],
        out_specs=vmem(),
        compiler_params=params(),
        cost_estimate=cost(0, 64 << 10),
    )(*blocks)


def expert_math(pieces, me, w_gate, w_up, w_down, experts, splits):
    blocks = sum(p.shape[0] for p in pieces)
    width, hid = w_gate.shape
    _, rows, full = pieces[0].shape
    lanes = full - width
    half = rows // 2
    m = blocks * half
    count = len(pieces)

    def body(*refs):
        me_ref, wg_ref, wu_ref, wd_ref = refs[count : count + 4]
        outs = refs[count + 4 :]
        parts, (t_ref, do_ref, h_ref, dg_ref, du_ref) = outs[: len(splits)], outs[len(splits) :]
        x = jnp.concatenate([r[...] for r in refs[:count]], axis=0)
        token = x[:, :half, :width].reshape(m, width)
        t_ref[...] = token
        side = x[:, :half, width:].reshape(m, lanes).astype(F32)
        lane = lax.broadcasted_iota(jnp.int32, (1, lanes), 1)
        mine = me_ref[0]
        scale = jnp.where(lane == mine, 1.0 / 256.0, 0.0) + jnp.where(lane == mine + experts, 1.0 / 65536.0, 0.0)
        coef = jnp.sum(side * scale, axis=1, keepdims=True)
        dout = (coef * x[:, half:, :width].reshape(m, width).astype(F32)).astype(BF16)
        do_ref[...] = dout
        gate = dot(token, wg_ref[...])
        upper = dot(token, wu_ref[...])
        dact = dot(dout, wd_ref[...], 1, 1)
        sig = jax.nn.sigmoid(gate)
        swish = gate * sig
        hidden = (swish * upper).astype(BF16)
        dgate = (dact * upper * sig * (1.0 + gate * (1.0 - sig))).astype(BF16)
        dupper = (dact * swish).astype(BF16)
        h_ref[...], dg_ref[...], du_ref[...] = hidden, dgate, dupper
        part = (coef * dot(hidden, wd_ref[...])).astype(BF16).reshape(blocks, half, width)
        back = dot(dgate, wg_ref[...], 1, 1) + dot(dupper, wu_ref[...], 1, 1)
        back = back.astype(BF16).reshape(blocks, half, width)
        at = 0
        for ref, n in zip(parts, splits):
            ref[:, :half] = part[at : at + n]
            ref[:, half:] = back[at : at + n]
            at += n

    outs = [shape(n, rows, width) for n in splits]
    outs += [shape(m, width), shape(m, width), shape(m, hid), shape(m, hid), shape(m, hid)]
    got = pl.pallas_call(
        body,
        out_shape=outs,
        in_specs=[vmem()] * count + [pl.BlockSpec(memory_space=pltpu.SMEM)] + [vmem()] * 3,
        out_specs=[vmem() for _ in outs],
        compiler_params=params(),
        cost_estimate=cost(12 * m * width * hid, 10 << 20),
    )(*pieces, me, w_gate, w_up, w_down)
    return list(got[: len(splits)]), got[len(splits) :]


def weight_grads(left, rights, steps):
    m, rows = left.shape
    cols = rights[0].shape[1]
    steps = steps if rows % (128 * steps) == 0 else 1
    tile = rows // steps

    def body(l_ref, *refs):
        for r_ref, o_ref in zip(refs[: len(rights)], refs[len(rights) :]):
            o_ref[...] = dot(l_ref[...], r_ref[...], 0, 0).astype(BF16)

    return pl.pallas_call(
        body,
        grid=(steps,),
        out_shape=[shape(rows, cols) for _ in rights],
        in_specs=[pl.BlockSpec((m, tile), lambda i: (0, i))] + [pl.BlockSpec((m, cols), lambda i: (0, 0)) for _ in rights],
        out_specs=[pl.BlockSpec((tile, cols), lambda i: (i, 0)) for _ in rights],
        compiler_params=params(),
        cost_estimate=cost(2 * m * rows * cols * len(rights), 2 * rows * cols * len(rights)),
    )(left, *rights)


def add(terms, splits):
    outs = [shape(n, *terms[0].shape[1:], dtype=BF16 if i else F32) for i, n in enumerate(splits)]

    def body(*refs):
        total = sum(r[...].astype(F32) for r in refs[: len(terms)])
        at = 0
        for ref, n in zip(refs[len(terms) :], splits):
            ref[...] = total[at : at + n].astype(ref.dtype)
            at += n

    return pl.pallas_call(
        body,
        out_shape=outs,
        in_specs=[vmem() for _ in terms],
        out_specs=[vmem() for _ in outs],
        compiler_params=params(),
        cost_estimate=cost(0, 64 << 10),
    )(*terms)


def add_ungroup(terms, after):
    _, rows, width = terms[0].shape
    outs = [shape(1, 2 * ROWS, width, dtype=BF16 if i else F32) for i in range(GROUP)]

    def body(*refs):
        total = sum(r[...].astype(F32) for r in refs[: len(terms)])[0]
        low = lax.broadcasted_iota(jnp.int32, (2 * ROWS, 1), 0) < ROWS
        for i, ref in enumerate(refs[-GROUP:]):
            at = i // 2 * 2 * ROWS
            out, back = total[at : at + 2 * ROWS], total[rows // 2 + at : rows // 2 + at + 2 * ROWS]
            if i % 2:
                block = jnp.where(low, pltpu.roll(out, ROWS, 0), back)
            else:
                block = jnp.where(low, out, pltpu.roll(back, ROWS, 0))
            ref[0] = block.astype(ref.dtype)

    return pl.pallas_call(
        body,
        out_shape=outs,
        in_specs=[vmem() for _ in terms] + [hbm() for _ in after],
        out_specs=[vmem() for _ in outs],
        compiler_params=params(),
        cost_estimate=cost(0, 64 << 10),
    )(*terms, *outside(after))


def add_pair(one, two):
    def body(a_ref, b_ref, o_ref):
        o_ref[...] = (a_ref[...].astype(F32) + b_ref[...].astype(F32)).astype(BF16)

    return pl.pallas_call(
        body,
        out_shape=shape(*one.shape),
        in_specs=[vmem(), vmem()],
        out_specs=vmem(),
        compiler_params=params(),
        cost_estimate=cost(0, 64 << 10),
    )(one, two)


def finish(terms, after=()):
    _, _, width = terms[0].shape

    def body(*refs):
        total = refs[0][...].astype(F32)
        for r in refs[1 : len(terms)]:
            total += r[...].astype(F32)
        out_ref, back_ref = refs[len(terms) + len(after) :]
        out_ref[...] = total[0, :ROWS].astype(BF16)
        back_ref[...] = total[0, ROWS:].astype(BF16)

    return pl.pallas_call(
        body,
        out_shape=[shape(ROWS, width)] * 2,
        in_specs=[vmem() for _ in terms] + [hbm() for _ in after],
        out_specs=[vmem(), vmem()],
        compiler_params=params(),
        cost_estimate=cost(0, 64 << 10),
    )(*terms, *outside(after))


def on_device(tokens, route_ids, route_weights, w_gate, w_up, w_down, grad_out):
    experts = w_gate.shape[0] * lax.axis_size("expert")
    core = lax.axis_size("dp")
    total = lax.axis_size("expert") * core
    plan = stages(total, core)
    me = lax.axis_index("expert").astype(jnp.int32).reshape(1)
    wg, wu, wd = w_gate[0], w_up[0], w_down[0]

    block = pack(tokens, route_ids, route_weights, grad_out, experts)
    block = regroup([block] + [exchange(block, mask, total, core) for mask in plan[0]])
    for masks in plan[1:]:
        held = [block] + [exchange(block, mask, total, core) for mask in masks]
        block = jnp.concatenate(held, axis=0)
    wg, wu, wd = fetch((wg, wu, wd), held[0])
    own, wg, wu, wd = lax.optimization_barrier((held[0], wg, wu, wd))
    pieces = held + [exchange(h, (core, core), total, core) for h in [own] + held[1:]]

    ways = len(held)
    groups = total // GROUP
    size = groups // 2 // ways
    if groups <= CHUNK:
        parts, kept = expert_math(pieces, me, wg, wu, wd, experts, [size] * (2 * ways))
    else:
        whole = jnp.concatenate(pieces, axis=0)
        sums, saved = [], []
        for at in range(0, groups, CHUNK):
            (got,), rest = expert_math([whole[at : at + CHUNK]], me, wg, wu, wd, experts, [CHUNK])
            sums.append(got)
            saved.append(rest)
        got = jnp.concatenate(sums, axis=0)
        parts = [got[at : at + size] for at in range(0, groups, size)]
        kept = [jnp.concatenate(p, axis=0) for p in zip(*saved)]
    token, dout, hidden, dgate, dupper = kept

    gate_grad, up_grad = weight_grads(token, [dgate, dupper], 2)
    (down_grad,) = weight_grads(hidden, [dout], 2)

    keep, send = parts[:ways], parts[ways:]
    arrived = [exchange(p, (core, core), total, core) for p in send]
    terms = [keep[0], arrived[0]]
    for at, mask in enumerate(plan[-1]):
        terms.append(exchange(add_pair(keep[at + 1], arrived[at + 1]), mask, total, core))
    for masks in reversed(plan[1:-1]):
        ways = len(masks) + 1
        mine, *others = add(terms, [terms[0].shape[0] // ways] * ways)
        terms = [mine] + [exchange(o, mask, total, core) for o, mask in zip(others, masks)]
    mine, *others = add_ungroup(terms, (gate_grad,))
    terms = [mine] + [exchange(o, mask, total, core) for o, mask in zip(others, plan[0])]
    mixed, back = finish(terms, (down_grad,))
    return mixed, back, gate_grad[None], up_grad[None], down_grad[None]


def solution(mesh):
    rows = P(("groups", "expert", "dp"), None)
    in_specs = (rows, rows, rows, P("expert", None, "dp"), P("expert", None, "dp"), P("expert", "dp", None), rows)
    hidden = P(("groups", "expert"), None, "dp")
    out_specs = (rows, rows, hidden, hidden, P(("groups", "expert"), "dp", None))
    return jax.shard_map(on_device, mesh=mesh, in_specs=in_specs, out_specs=out_specs, check_vma=False)
```

```python
import jax
import jax.numpy as jnp
from jax import lax
from jax.experimental import pallas as pl
from jax.experimental.pallas import tpu as pltpu
from jax.sharding import PartitionSpec as P

AXES = ("expert", "dp")
ROWS = 4
GROUP = 4
CHUNK = 8
LARGE = 16 * 1024 * 1024
SMALL = 4 * 1024 * 1024
F32 = jnp.float32
BF16 = jnp.bfloat16


def vmem():
    return pl.BlockSpec(memory_space=pltpu.VMEM)


def hbm():
    return pl.BlockSpec(memory_space=pltpu.HBM)


def outside(arrays):
    return [pltpu.with_memory_space_constraint(a, pltpu.HBM) for a in arrays]


def shape(*dims, dtype=BF16):
    return jax.ShapeDtypeStruct(dims, dtype)


def params(limit=SMALL):
    return pltpu.CompilerParams(vmem_limit_bytes=limit)


def cost(flops, moved):
    return pl.CostEstimate(flops=flops, bytes_accessed=moved, transcendentals=0)


def dot(a, b, ca=1, cb=0):
    return lax.dot_general(a, b, (((ca,), (cb,)), ((), ())), preferred_element_type=F32)


def exchange(x, masks, total, core):
    return lax.ppermute(x, AXES, [(i, i ^ masks[i // core % 2]) for i in range(total)])


def stages(total, core):
    bits = [1 << b for b in reversed(range(total.bit_length() - 1)) if 1 << b != core]
    plan = []
    while bits:
        a, bits = bits[0], bits[1:]
        if not bits:
            plan.append([(a, a)])
            continue
        b, bits = bits[0], bits[1:]
        if (a > core) == (b > core) and b > 2 * core:
            plan.append([(b, b), (a, a), (a + b, a + b)])
        else:
            plan.append([(b, a), (a, b), (a + b, a + b)])
    return plan


def pack(tokens, route_ids, route_weights, grad_out, experts):
    rows, width = tokens.shape
    lanes = -(-2 * experts // 128) * 128

    def body(t_in, i_in, w_in, g_in, o_ref, t_ref, i_ref, w_ref, g_ref, sems):
        pairs = ((t_in, t_ref), (i_in, i_ref), (w_in, w_ref), (g_in, g_ref))
        copies = [pltpu.make_async_copy(a, b, sems.at[k]) for k, (a, b) in enumerate(pairs)]
        for c in copies:
            c.start()
        for c in copies:
            c.wait()
        lane = lax.broadcasted_iota(jnp.int32, (rows, lanes), 1)
        ids, weights = i_ref[...], w_ref[...]
        coded = jnp.zeros((rows, lanes), jnp.int32)
        for k in range(ids.shape[1]):
            one, w = ids[:, k : k + 1], weights[:, k : k + 1]
            coded += jnp.where(lane == one, w >> 8, 0) + jnp.where(lane == one + experts, w & 255, 0)
        both = jnp.concatenate([t_ref[...].astype(F32), g_ref[...].astype(F32)], axis=0)
        side = jnp.concatenate([coded.astype(F32), jnp.zeros((rows, lanes), F32)], axis=0)
        o_ref[0] = jnp.concatenate([both, side], axis=1).astype(BF16)

    args = (tokens, route_ids, route_weights, grad_out)
    return pl.pallas_call(
        body,
        out_shape=shape(1, 2 * rows, width + lanes),
        in_specs=[hbm() for _ in args],
        out_specs=vmem(),
        scratch_shapes=[pltpu.VMEM(a.shape, a.dtype) for a in args] + [pltpu.SemaphoreType.DMA((len(args),))],
        compiler_params=params(),
        cost_estimate=cost(0, 80 << 10),
    )(*outside(args))


def fetch(w, block):
    def body(w_ref, b_ref, o_ref, c_ref, sem):
        copy = pltpu.make_async_copy(w_ref, o_ref, sem)
        copy.start()
        c_ref[...] = b_ref[...]
        copy.wait()

    return pl.pallas_call(
        body,
        out_shape=[shape(*w.shape), shape(*block.shape)],
        in_specs=[hbm(), vmem()],
        out_specs=[vmem(), vmem()],
        scratch_shapes=[pltpu.SemaphoreType.DMA],
        compiler_params=params(),
        cost_estimate=cost(0, 4 << 20),
    )(*outside((w,)), block)


def fetch_behind(w_down, w_up, after):
    rows = w_up.shape[0] // 2

    def body(d_ref, u_ref, _, od_ref, ou_ref, sems):
        copies = [
            pltpu.make_async_copy(d_ref, od_ref, sems.at[0]),
            pltpu.make_async_copy(u_ref.at[:rows], ou_ref, sems.at[1]),
        ]
        for c in copies:
            c.start()
        for c in copies:
            c.wait()

    return pl.pallas_call(
        body,
        out_shape=[shape(*w_down.shape), shape(rows, w_up.shape[1])],
        in_specs=[hbm(), hbm(), pl.BlockSpec(memory_space=pl.ANY)],
        out_specs=[vmem(), vmem()],
        scratch_shapes=[pltpu.SemaphoreType.DMA((2,))],
        compiler_params=params(),
        cost_estimate=cost(0, 6 << 20),
    )(*outside((w_down, w_up)), after)


def regroup(blocks):
    _, rows, width = blocks[0].shape

    def body(*refs):
        x = [r[0].astype(F32) for r in refs[:-1]]
        low = lax.broadcasted_iota(jnp.int32, (rows, 1), 0) < ROWS
        pairs = list(zip(x[::2], x[1::2]))
        token = [jnp.where(low, a, pltpu.roll(b, ROWS, 0)) for a, b in pairs]
        grads = [jnp.where(low, pltpu.roll(a, ROWS, 0), b) for a, b in pairs]
        refs[-1][0] = jnp.concatenate(token + grads, axis=0).astype(BF16)

    return pl.pallas_call(
        body,
        out_shape=shape(1, rows * len(blocks), width),
        in_specs=[vmem() for _ in blocks],
        out_specs=vmem(),
        compiler_params=params(),
        cost_estimate=cost(0, 64 << 10),
    )(*blocks)


def expert_math(pieces, me, w_gate, w_down, w_first, w_up, experts, splits):
    blocks = sum(p.shape[0] for p in pieces)
    hid, width = w_down.shape
    _, rows, full = pieces[0].shape
    lanes = full - width
    half = rows // 2
    m = blocks * half
    count = len(pieces)

    def body(*refs):
        me_ref, wg_ref, wd_ref, wu_ref, up_in = refs[count : count + 5]
        outs = refs[count + 5 : -5]
        late_ref, gate_ref, upper_ref, dact_ref, sem = refs[-5:]
        parts, (t_ref, do_ref, h_ref, dg_ref, du_ref) = outs[: len(splits)], outs[len(splits) :]
        copy = pltpu.make_async_copy(up_in.at[width // 2 :], late_ref, sem)
        copy.start()
        x = jnp.concatenate([r[...] for r in refs[:count]], axis=0)
        t_ref[...] = x[:, :half, :width].reshape(m, width)
        gate_ref[...] = dot(t_ref[...], wg_ref[...])
        side = x[:, :half, width:].reshape(m, lanes).astype(F32)
        lane = lax.broadcasted_iota(jnp.int32, (1, lanes), 1)
        mine = me_ref[0]
        scale = jnp.where(lane == mine, 1.0 / 256.0, 0.0) + jnp.where(lane == mine + experts, 1.0 / 65536.0, 0.0)
        coef = jnp.sum(side * scale, axis=1, keepdims=True)
        do_ref[...] = (coef * x[:, half:, :width].reshape(m, width).astype(F32)).astype(BF16)
        dact_ref[...] = dot(do_ref[...], wd_ref[...], 1, 1)
        upper_ref[...] = dot(t_ref[:, : width // 2], wu_ref[...])
        copy.wait()
        gate, dact = gate_ref[...], dact_ref[...]
        upper = upper_ref[...] + dot(t_ref[:, width // 2 :], late_ref[...])
        sig = jax.nn.sigmoid(gate)
        swish = gate * sig
        hidden = (swish * upper).astype(BF16)
        dgate = (dact * upper * sig * (1.0 + gate * (1.0 - sig))).astype(BF16)
        dupper = (dact * swish).astype(BF16)
        h_ref[...], dg_ref[...], du_ref[...] = hidden, dgate, dupper
        part = (coef * dot(hidden, wd_ref[...])).astype(BF16).reshape(blocks, half, width)
        back = jnp.concatenate([dot(dupper, w[...], 1, 1) for w in (wu_ref, late_ref)], axis=1)
        back = dot(dgate, wg_ref[...], 1, 1) + back
        back = back.astype(BF16).reshape(blocks, half, width)
        at = 0
        for ref, n in zip(parts, splits):
            ref[:, :half] = part[at : at + n]
            ref[:, half:] = back[at : at + n]
            at += n

    outs = [shape(n, rows, width) for n in splits]
    outs += [shape(m, width), shape(m, width), shape(m, hid), shape(m, hid), shape(m, hid)]
    got = pl.pallas_call(
        body,
        out_shape=outs,
        in_specs=[vmem()] * count + [pl.BlockSpec(memory_space=pltpu.SMEM)] + [vmem()] * 3 + [hbm()],
        out_specs=[vmem() for _ in outs],
        scratch_shapes=[
            pltpu.VMEM((width // 2, hid), BF16),
            pltpu.VMEM((m, hid), F32),
            pltpu.VMEM((m, hid), F32),
            pltpu.VMEM((m, hid), F32),
            pltpu.SemaphoreType.DMA,
        ],
        compiler_params=params(LARGE),
        cost_estimate=cost(12 * m * width * hid, 10 << 20),
    )(*pieces, me, w_gate, w_down, w_first, *outside((w_up,)))
    return list(got[: len(splits)]), got[len(splits) :]


def weight_grads(left, rights, steps):
    m, rows = left.shape
    cols = rights[0].shape[1]
    steps = steps if rows % (128 * steps) == 0 else 1
    tile = rows // steps

    def body(l_ref, *refs):
        for r_ref, o_ref in zip(refs[: len(rights)], refs[len(rights) :]):
            o_ref[...] = dot(l_ref[...], r_ref[...], 0, 0).astype(BF16)

    return pl.pallas_call(
        body,
        grid=(steps,),
        out_shape=[shape(rows, cols) for _ in rights],
        in_specs=[pl.BlockSpec((m, tile), lambda i: (0, i))] + [pl.BlockSpec((m, cols), lambda i: (0, 0)) for _ in rights],
        out_specs=[pl.BlockSpec((tile, cols), lambda i: (i, 0)) for _ in rights],
        compiler_params=params(LARGE),
        cost_estimate=cost(2 * m * rows * cols * len(rights), 2 * rows * cols * len(rights)),
    )(left, *rights)


def add(terms, splits):
    outs = [shape(n, *terms[0].shape[1:], dtype=BF16 if i else F32) for i, n in enumerate(splits)]

    def body(*refs):
        total = sum(r[...].astype(F32) for r in refs[: len(terms)])
        at = 0
        for ref, n in zip(refs[len(terms) :], splits):
            ref[...] = total[at : at + n].astype(ref.dtype)
            at += n

    return pl.pallas_call(
        body,
        out_shape=outs,
        in_specs=[vmem() for _ in terms],
        out_specs=[vmem() for _ in outs],
        compiler_params=params(),
        cost_estimate=cost(0, 64 << 10),
    )(*terms)


def add_ungroup(terms, after):
    _, rows, width = terms[0].shape
    outs = [shape(1, 2 * ROWS, width, dtype=BF16 if i else F32) for i in range(GROUP)]

    def body(*refs):
        total = sum(r[...].astype(F32) for r in refs[: len(terms)])[0]
        low = lax.broadcasted_iota(jnp.int32, (2 * ROWS, 1), 0) < ROWS
        for i, ref in enumerate(refs[-GROUP:]):
            at = i // 2 * 2 * ROWS
            out, back = total[at : at + 2 * ROWS], total[rows // 2 + at : rows // 2 + at + 2 * ROWS]
            if i % 2:
                block = jnp.where(low, pltpu.roll(out, ROWS, 0), back)
            else:
                block = jnp.where(low, out, pltpu.roll(back, ROWS, 0))
            ref[0] = block.astype(ref.dtype)

    return pl.pallas_call(
        body,
        out_shape=outs,
        in_specs=[vmem() for _ in terms] + [hbm() for _ in after],
        out_specs=[vmem() for _ in outs],
        compiler_params=params(),
        cost_estimate=cost(0, 64 << 10),
    )(*terms, *outside(after))


def add_pair(one, two):
    def body(a_ref, b_ref, o_ref):
        o_ref[...] = (a_ref[...].astype(F32) + b_ref[...].astype(F32)).astype(BF16)

    return pl.pallas_call(
        body,
        out_shape=shape(*one.shape),
        in_specs=[vmem(), vmem()],
        out_specs=vmem(),
        compiler_params=params(),
        cost_estimate=cost(0, 64 << 10),
    )(one, two)


def finish(terms, after=()):
    _, _, width = terms[0].shape

    def body(*refs):
        total = refs[0][...].astype(F32)
        for r in refs[1 : len(terms)]:
            total += r[...].astype(F32)
        out_ref, back_ref = refs[len(terms) + len(after) :]
        out_ref[...] = total[0, :ROWS].astype(BF16)
        back_ref[...] = total[0, ROWS:].astype(BF16)

    return pl.pallas_call(
        body,
        out_shape=[shape(ROWS, width)] * 2,
        in_specs=[vmem() for _ in terms] + [hbm() for _ in after],
        out_specs=[vmem(), vmem()],
        compiler_params=params(),
        cost_estimate=cost(0, 64 << 10),
    )(*terms, *outside(after))


def on_device(tokens, route_ids, route_weights, w_gate, w_up, w_down, grad_out):
    experts = w_gate.shape[0] * lax.axis_size("expert")
    core = lax.axis_size("dp")
    total = lax.axis_size("expert") * core
    plan = stages(total, core)
    me = lax.axis_index("expert").astype(jnp.int32).reshape(1)
    wg, wu, wd = w_gate[0], w_up[0], w_down[0]

    block = pack(tokens, route_ids, route_weights, grad_out, experts)
    block = regroup([block] + [exchange(block, mask, total, core) for mask in plan[0]])
    for masks in plan[1:]:
        held = [block] + [exchange(block, mask, total, core) for mask in masks]
        block = jnp.concatenate(held, axis=0)
    wg, own = fetch(wg, held[0])
    wd, wu_first = fetch_behind(wd, wu, held[1])
    pieces = held + [exchange(h, (core, core), total, core) for h in [own] + held[1:]]

    ways = len(held)
    groups = total // GROUP
    size = groups // 2 // ways
    if groups <= CHUNK:
        parts, kept = expert_math(pieces, me, wg, wd, wu_first, wu, experts, [size] * (2 * ways))
    else:
        whole = jnp.concatenate(pieces, axis=0)
        sums, saved = [], []
        for at in range(0, groups, CHUNK):
            (got,), rest = expert_math([whole[at : at + CHUNK]], me, wg, wd, wu_first, wu, experts, [CHUNK])
            sums.append(got)
            saved.append(rest)
        got = jnp.concatenate(sums, axis=0)
        parts = [got[at : at + size] for at in range(0, groups, size)]
        kept = [jnp.concatenate(p, axis=0) for p in zip(*saved)]
    token, dout, hidden, dgate, dupper = kept

    gate_grad, up_grad = weight_grads(token, [dgate, dupper], 2)
    (down_grad,) = weight_grads(hidden, [dout], 2)

    keep, send = parts[:ways], parts[ways:]
    arrived = [exchange(p, (core, core), total, core) for p in send[::-1]][::-1]
    terms = []
    for at, mask in reversed(list(enumerate(plan[-1]))):
        terms.append(exchange(add_pair(keep[at + 1], arrived[at + 1]), mask, total, core))
    terms += [keep[0], arrived[0]]
    for masks in reversed(plan[1:-1]):
        ways = len(masks) + 1
        mine, *others = add(terms, [terms[0].shape[0] // ways] * ways)
        terms = [mine] + [exchange(o, mask, total, core) for o, mask in zip(others[::-1], masks[::-1])]
    mine, *others = add_ungroup(terms, (gate_grad,))
    terms = [mine] + [exchange(o, mask, total, core) for o, mask in zip(others[::-1], plan[0][::-1])]
    mixed, back = finish(terms, (down_grad,))
    return mixed, back, gate_grad[None], up_grad[None], down_grad[None]


def solution(mesh):
    rows = P(("groups", "expert", "dp"), None)
    in_specs = (rows, rows, rows, P("expert", None, "dp"), P("expert", None, "dp"), P("expert", "dp", None), rows)
    hidden = P(("groups", "expert"), None, "dp")
    out_specs = (rows, rows, hidden, hidden, P(("groups", "expert"), "dp", None))
    return jax.shard_map(on_device, mesh=mesh, in_specs=in_specs, out_specs=out_specs, check_vma=False)
```

```python
import jax
import jax.numpy as jnp
from jax import lax
from jax.experimental import pallas as pl
from jax.experimental.pallas import tpu as pltpu
from jax.sharding import PartitionSpec as P

AXES = ("expert", "dp")
ROWS = 4
GROUP = 4
CHUNK = 8
LARGE = 16 * 1024 * 1024
SMALL = 4 * 1024 * 1024
GATHER_FIRST = (0, 1, 2)
GATHER_LAST = (0, 1, 2)
CORE_ORDER = (3, 2, 1, 0)
SCATTER_FIRST = (2, 1, 0)
SCATTER_LAST = (2, 1, 0)
F32 = jnp.float32
BF16 = jnp.bfloat16


def vmem():
    return pl.BlockSpec(memory_space=pltpu.VMEM)


def hbm():
    return pl.BlockSpec(memory_space=pltpu.HBM)


def outside(arrays):
    return [pltpu.with_memory_space_constraint(a, pltpu.HBM) for a in arrays]


def shape(*dims, dtype=BF16):
    return jax.ShapeDtypeStruct(dims, dtype)


def params(limit=SMALL):
    return pltpu.CompilerParams(vmem_limit_bytes=limit)


def cost(flops, moved):
    return pl.CostEstimate(flops=flops, bytes_accessed=moved, transcendentals=0)


def dot(a, b, ca=1, cb=0):
    return lax.dot_general(a, b, (((ca,), (cb,)), ((), ())), preferred_element_type=F32)


def exchange(x, masks, total, core):
    return lax.ppermute(x, AXES, [(i, i ^ masks[i // core % 2]) for i in range(total)])


def exchange_all(blocks, masks, order, total, core):
    got = {}
    for at in order:
        if at < len(masks):
            block = blocks[at] if isinstance(blocks, list) else blocks
            got[at] = exchange(block, masks[at], total, core)
    return got


def stages(total, core):
    bits = [1 << b for b in reversed(range(total.bit_length() - 1)) if 1 << b != core]
    plan = []
    while bits:
        a, bits = bits[0], bits[1:]
        if not bits:
            plan.append([(a, a)])
            continue
        b, bits = bits[0], bits[1:]
        if (a > core) == (b > core) and b > 2 * core:
            plan.append([(b, b), (a, a), (a + b, a + b)])
        else:
            plan.append([(b, a), (a, b), (a + b, a + b)])
    return plan


def pack(tokens, route_ids, route_weights, grad_out, experts):
    rows, width = tokens.shape
    lanes = -(-2 * experts // 128) * 128

    def body(t_in, i_in, w_in, g_in, o_ref, t_ref, i_ref, w_ref, g_ref, sems):
        pairs = ((t_in, t_ref), (i_in, i_ref), (w_in, w_ref), (g_in, g_ref))
        copies = [pltpu.make_async_copy(a, b, sems.at[k]) for k, (a, b) in enumerate(pairs)]
        for c in copies:
            c.start()
        for c in copies:
            c.wait()
        lane = lax.broadcasted_iota(jnp.int32, (rows, lanes), 1)
        ids, weights = i_ref[...], w_ref[...]
        coded = jnp.zeros((rows, lanes), jnp.int32)
        for k in range(ids.shape[1]):
            one, w = ids[:, k : k + 1], weights[:, k : k + 1]
            coded += jnp.where(lane == one, w >> 8, 0) + jnp.where(lane == one + experts, w & 255, 0)
        both = jnp.concatenate([t_ref[...].astype(F32), g_ref[...].astype(F32)], axis=0)
        side = jnp.concatenate([coded.astype(F32), jnp.zeros((rows, lanes), F32)], axis=0)
        o_ref[0] = jnp.concatenate([both, side], axis=1).astype(BF16)

    args = (tokens, route_ids, route_weights, grad_out)
    return pl.pallas_call(
        body,
        out_shape=shape(1, 2 * rows, width + lanes),
        in_specs=[hbm() for _ in args],
        out_specs=vmem(),
        scratch_shapes=[pltpu.VMEM(a.shape, a.dtype) for a in args] + [pltpu.SemaphoreType.DMA((len(args),))],
        compiler_params=params(),
        cost_estimate=cost(0, 80 << 10),
    )(*outside(args))


def fetch(w, block):
    def body(w_ref, b_ref, o_ref, c_ref, sem):
        copy = pltpu.make_async_copy(w_ref, o_ref, sem)
        copy.start()
        c_ref[...] = b_ref[...]
        copy.wait()

    return pl.pallas_call(
        body,
        out_shape=[shape(*w.shape), shape(*block.shape)],
        in_specs=[hbm(), vmem()],
        out_specs=[vmem(), vmem()],
        scratch_shapes=[pltpu.SemaphoreType.DMA],
        compiler_params=params(),
        cost_estimate=cost(0, 4 << 20),
    )(*outside((w,)), block)


def fetch_behind(weights, after):
    n = len(weights)

    def body(*refs):
        copies = [pltpu.make_async_copy(refs[k], refs[n + 1 + k], refs[-1].at[k]) for k in range(n)]
        for c in copies:
            c.start()
        for c in copies:
            c.wait()

    return pl.pallas_call(
        body,
        out_shape=[shape(*w.shape) for w in weights],
        in_specs=[hbm() for _ in weights] + [pl.BlockSpec(memory_space=pl.ANY)],
        out_specs=[vmem() for _ in weights],
        scratch_shapes=[pltpu.SemaphoreType.DMA((n,))],
        compiler_params=params(),
        cost_estimate=cost(0, 8 << 20),
    )(*outside(weights), after)


def regroup(blocks, places):
    _, rows, width = blocks[0].shape

    def body(*refs):
        x = [refs[places.index(at)][0].astype(F32) for at in range(len(blocks))]
        low = lax.broadcasted_iota(jnp.int32, (rows, 1), 0) < ROWS
        pairs = list(zip(x[::2], x[1::2]))
        token = [jnp.where(low, a, pltpu.roll(b, ROWS, 0)) for a, b in pairs]
        grads = [jnp.where(low, pltpu.roll(a, ROWS, 0), b) for a, b in pairs]
        refs[-1][0] = jnp.concatenate(token + grads, axis=0).astype(BF16)

    return pl.pallas_call(
        body,
        out_shape=shape(1, rows * len(blocks), width),
        in_specs=[vmem() for _ in blocks],
        out_specs=vmem(),
        compiler_params=params(),
        cost_estimate=cost(0, 64 << 10),
    )(*blocks)


def expert_math(pieces, me, w_gate, w_up, w_down, experts, splits):
    blocks = sum(p.shape[0] for p in pieces)
    width, hid = w_gate.shape
    _, rows, full = pieces[0].shape
    lanes = full - width
    half = rows // 2
    m = blocks * half
    count = len(pieces)

    def body(*refs):
        me_ref, wg_ref, wu_ref, wd_ref = refs[count : count + 4]
        outs = refs[count + 4 :]
        parts, (t_ref, do_ref, h_ref, dg_ref, du_ref) = outs[: len(splits)], outs[len(splits) :]
        x = jnp.concatenate([r[...] for r in refs[:count]], axis=0)
        token = x[:, :half, :width].reshape(m, width)
        t_ref[...] = token
        side = x[:, :half, width:].reshape(m, lanes).astype(F32)
        lane = lax.broadcasted_iota(jnp.int32, (1, lanes), 1)
        mine = me_ref[0]
        scale = jnp.where(lane == mine, 1.0 / 256.0, 0.0) + jnp.where(lane == mine + experts, 1.0 / 65536.0, 0.0)
        coef = jnp.sum(side * scale, axis=1, keepdims=True)
        dout = (coef * x[:, half:, :width].reshape(m, width).astype(F32)).astype(BF16)
        do_ref[...] = dout
        gate = dot(token, wg_ref[...])
        upper = dot(token, wu_ref[...])
        dact = dot(dout, wd_ref[...], 1, 1)
        sig = jax.nn.sigmoid(gate)
        swish = gate * sig
        hidden = (swish * upper).astype(BF16)
        dgate = (dact * upper * sig * (1.0 + gate * (1.0 - sig))).astype(BF16)
        dupper = (dact * swish).astype(BF16)
        h_ref[...], dg_ref[...], du_ref[...] = hidden, dgate, dupper
        part = (coef * dot(hidden, wd_ref[...])).astype(BF16).reshape(blocks, half, width)
        back = dot(wg_ref[...], dgate, 1, 1) + dot(wu_ref[...], dupper, 1, 1)
        back = back.astype(BF16).T.reshape(blocks, half, width)
        at = 0
        for ref, n in zip(parts, splits):
            ref[:, :half] = part[at : at + n]
            ref[:, half:] = back[at : at + n]
            at += n

    outs = [shape(n, rows, width) for n in splits]
    outs += [shape(m, width), shape(m, width), shape(m, hid), shape(m, hid), shape(m, hid)]
    got = pl.pallas_call(
        body,
        out_shape=outs,
        in_specs=[vmem()] * count + [pl.BlockSpec(memory_space=pltpu.SMEM)] + [vmem()] * 3,
        out_specs=[vmem() for _ in outs],
        compiler_params=params(LARGE),
        cost_estimate=cost(12 * m * width * hid, 10 << 20),
    )(*pieces, me, w_gate, w_up, w_down)
    return list(got[: len(splits)]), got[len(splits) :]


def weight_grads(left, rights, steps):
    m, rows = left.shape
    cols = rights[0].shape[1]
    steps = steps if rows % (128 * steps) == 0 else 1
    tile = rows // steps

    def body(l_ref, *refs):
        for r_ref, o_ref in zip(refs[: len(rights)], refs[len(rights) :]):
            o_ref[...] = dot(l_ref[...], r_ref[...], 0, 0).astype(BF16)

    return pl.pallas_call(
        body,
        grid=(steps,),
        out_shape=[shape(rows, cols) for _ in rights],
        in_specs=[pl.BlockSpec((m, tile), lambda i: (0, i))] + [pl.BlockSpec((m, cols), lambda i: (0, 0)) for _ in rights],
        out_specs=[pl.BlockSpec((tile, cols), lambda i: (i, 0)) for _ in rights],
        compiler_params=params(LARGE),
        cost_estimate=cost(2 * m * rows * cols * len(rights), 2 * rows * cols * len(rights)),
    )(left, *rights)


def add(terms, splits):
    outs = [shape(n, *terms[0].shape[1:], dtype=BF16 if i else F32) for i, n in enumerate(splits)]

    def body(*refs):
        total = sum(r[...].astype(F32) for r in refs[: len(terms)])
        at = 0
        for ref, n in zip(refs[len(terms) :], splits):
            ref[...] = total[at : at + n].astype(ref.dtype)
            at += n

    return pl.pallas_call(
        body,
        out_shape=outs,
        in_specs=[vmem() for _ in terms],
        out_specs=[vmem() for _ in outs],
        compiler_params=params(),
        cost_estimate=cost(0, 64 << 10),
    )(*terms)


def add_ungroup(terms, after):
    _, rows, width = terms[0].shape
    outs = [shape(1, 2 * ROWS, width, dtype=BF16 if i else F32) for i in range(GROUP)]

    def body(*refs):
        total = sum(r[...].astype(F32) for r in refs[: len(terms)])[0]
        low = lax.broadcasted_iota(jnp.int32, (2 * ROWS, 1), 0) < ROWS
        for i, ref in enumerate(refs[-GROUP:]):
            at = i // 2 * 2 * ROWS
            out, back = total[at : at + 2 * ROWS], total[rows // 2 + at : rows // 2 + at + 2 * ROWS]
            if i % 2:
                block = jnp.where(low, pltpu.roll(out, ROWS, 0), back)
            else:
                block = jnp.where(low, out, pltpu.roll(back, ROWS, 0))
            ref[0] = block.astype(ref.dtype)

    return pl.pallas_call(
        body,
        out_shape=outs,
        in_specs=[vmem() for _ in terms] + [hbm() for _ in after],
        out_specs=[vmem() for _ in outs],
        compiler_params=params(),
        cost_estimate=cost(0, 64 << 10),
    )(*terms, *outside(after))


def add_pair(one, two):
    def body(a_ref, b_ref, o_ref):
        o_ref[...] = (a_ref[...].astype(F32) + b_ref[...].astype(F32)).astype(BF16)

    return pl.pallas_call(
        body,
        out_shape=shape(*one.shape),
        in_specs=[vmem(), vmem()],
        out_specs=vmem(),
        compiler_params=params(),
        cost_estimate=cost(0, 64 << 10),
    )(one, two)


def finish(terms, after=()):
    _, _, width = terms[0].shape

    def body(*refs):
        total = refs[0][...].astype(F32)
        for r in refs[1 : len(terms)]:
            total += r[...].astype(F32)
        out_ref, back_ref = refs[len(terms) + len(after) :]
        out_ref[...] = total[0, :ROWS].astype(BF16)
        back_ref[...] = total[0, ROWS:].astype(BF16)

    return pl.pallas_call(
        body,
        out_shape=[shape(ROWS, width)] * 2,
        in_specs=[vmem() for _ in terms] + [hbm() for _ in after],
        out_specs=[vmem(), vmem()],
        compiler_params=params(),
        cost_estimate=cost(0, 64 << 10),
    )(*terms, *outside(after))


def on_device(tokens, route_ids, route_weights, w_gate, w_up, w_down, grad_out):
    experts = w_gate.shape[0] * lax.axis_size("expert")
    core = lax.axis_size("dp")
    total = lax.axis_size("expert") * core
    plan = stages(total, core)
    me = lax.axis_index("expert").astype(jnp.int32).reshape(1)
    wg, wu, wd = w_gate[0], w_up[0], w_down[0]

    block = pack(tokens, route_ids, route_weights, grad_out, experts)
    got = exchange_all(block, plan[0], GATHER_FIRST, total, core)
    block = regroup([block, *got.values()], [0] + [at + 1 for at in got])
    for masks in plan[1:]:
        got = exchange_all(block, masks, GATHER_LAST, total, core)
        held = [block] + [got[at] for at in range(len(masks))]
        block = jnp.concatenate(held, axis=0)
    wg, own = fetch(wg, held[0])
    wu, wd = fetch_behind((wu, wd), held[1])
    pieces = held + [exchange(h, (core, core), total, core) for h in [own] + held[1:]]

    ways = len(held)
    groups = total // GROUP
    size = groups // 2 // ways
    if groups <= CHUNK:
        parts, kept = expert_math(pieces, me, wg, wu, wd, experts, [size] * (2 * ways))
    else:
        whole = jnp.concatenate(pieces, axis=0)
        sums, saved = [], []
        for at in range(0, groups, CHUNK):
            (got,), rest = expert_math([whole[at : at + CHUNK]], me, wg, wu, wd, experts, [CHUNK])
            sums.append(got)
            saved.append(rest)
        got = jnp.concatenate(sums, axis=0)
        parts = [got[at : at + size] for at in range(0, groups, size)]
        kept = [jnp.concatenate(p, axis=0) for p in zip(*saved)]
    token, dout, hidden, dgate, dupper = kept

    gate_grad, up_grad = weight_grads(token, [dgate, dupper], 2)
    (down_grad,) = weight_grads(hidden, [dout], 2)

    keep, send = parts[:ways], parts[ways:]
    arrived = [exchange(send[at], (core, core), total, core) for at in CORE_ORDER if at < ways]
    arrived = dict(zip([at for at in CORE_ORDER if at < ways], arrived))
    sums = [add_pair(keep[at], arrived[at]) for at in range(1, ways)]
    terms = [*exchange_all(sums, plan[-1], SCATTER_FIRST, total, core).values(), keep[0], arrived[0]]
    for masks in reversed(plan[1:-1]):
        ways = len(masks) + 1
        mine, *others = add(terms, [terms[0].shape[0] // ways] * ways)
        terms = [mine, *exchange_all(others, masks, SCATTER_FIRST, total, core).values()]
    mine, *others = add_ungroup(terms, (gate_grad,))
    terms = [mine, *exchange_all(others, plan[0], SCATTER_LAST, total, core).values()]
    mixed, back = finish(terms, (down_grad,))
    return mixed, back, gate_grad[None], up_grad[None], down_grad[None]


def solution(mesh):
    rows = P(("groups", "expert", "dp"), None)
    in_specs = (rows, rows, rows, P("expert", None, "dp"), P("expert", None, "dp"), P("expert", "dp", None), rows)
    hidden = P(("groups", "expert"), None, "dp")
    out_specs = (rows, rows, hidden, hidden, P(("groups", "expert"), "dp", None))
    return jax.shard_map(on_device, mesh=mesh, in_specs=in_specs, out_specs=out_specs, check_vma=False)
```

```python
import jax
import jax.numpy as jnp
from jax import lax
from jax.experimental import pallas as pl
from jax.experimental.pallas import tpu as pltpu
from jax.sharding import PartitionSpec as P

AXES = ("expert", "dp")
ROWS = 4
GROUP = 4
CHUNK = 8
LARGE = 16 * 1024 * 1024
SMALL = 4 * 1024 * 1024
F32 = jnp.float32
BF16 = jnp.bfloat16


def vmem():
    return pl.BlockSpec(memory_space=pltpu.VMEM)


def hbm():
    return pl.BlockSpec(memory_space=pltpu.HBM)


def outside(arrays):
    return [pltpu.with_memory_space_constraint(a, pltpu.HBM) for a in arrays]


def shape(*dims, dtype=BF16):
    return jax.ShapeDtypeStruct(dims, dtype)


def params(limit=SMALL):
    return pltpu.CompilerParams(vmem_limit_bytes=limit)


def cost(flops, moved):
    return pl.CostEstimate(flops=flops, bytes_accessed=moved, transcendentals=0)


def dot(a, b, ca=1, cb=0):
    return lax.dot_general(a, b, (((ca,), (cb,)), ((), ())), preferred_element_type=F32)


def exchange(x, mask, total):
    return lax.ppermute(x, AXES, [(i, i ^ mask) for i in range(total)])


def exchange_all(blocks, masks, total):
    if not isinstance(blocks, list):
        blocks = [blocks] * len(masks)
    return [exchange(block, mask, total) for block, mask in zip(blocks, masks)]


def stages(total, core):
    bits = [1 << b for b in reversed(range(total.bit_length() - 1)) if 1 << b != core]
    pairs = [bits[i : i + 2] for i in range(0, len(bits), 2)]
    return [[p[1], p[0], p[0] + p[1]] if len(p) == 2 else p for p in pairs]


def pack(tokens, route_ids, route_weights, grad_out, experts):
    rows, width = tokens.shape
    lanes = -(-2 * experts // 128) * 128

    def body(t_in, i_in, w_in, g_in, o_ref, t_ref, i_ref, w_ref, g_ref, sems):
        pairs = ((t_in, t_ref), (i_in, i_ref), (w_in, w_ref), (g_in, g_ref))
        copies = [pltpu.make_async_copy(a, b, sems.at[k]) for k, (a, b) in enumerate(pairs)]
        for c in copies:
            c.start()
        for c in copies:
            c.wait()
        lane = lax.broadcasted_iota(jnp.int32, (rows, lanes), 1)
        ids, weights = i_ref[...], w_ref[...]
        coded = jnp.zeros((rows, lanes), jnp.int32)
        for k in range(ids.shape[1]):
            one, w = ids[:, k : k + 1], weights[:, k : k + 1]
            coded += jnp.where(lane == one, w >> 8, 0) + jnp.where(lane == one + experts, w & 255, 0)
        both = jnp.concatenate([t_ref[...].astype(F32), g_ref[...].astype(F32)], axis=0)
        side = jnp.concatenate([coded.astype(F32), jnp.zeros((rows, lanes), F32)], axis=0)
        o_ref[0] = jnp.concatenate([both, side], axis=1).astype(BF16)

    args = (tokens, route_ids, route_weights, grad_out)
    return pl.pallas_call(
        body,
        out_shape=shape(1, 2 * rows, width + lanes),
        in_specs=[hbm() for _ in args],
        out_specs=vmem(),
        scratch_shapes=[pltpu.VMEM(a.shape, a.dtype) for a in args] + [pltpu.SemaphoreType.DMA((len(args),))],
        compiler_params=params(),
        cost_estimate=cost(0, 80 << 10),
    )(*outside(args))


def fetch(w, block):
    def body(w_ref, b_ref, o_ref, c_ref, sem):
        copy = pltpu.make_async_copy(w_ref, o_ref, sem)
        copy.start()
        c_ref[...] = b_ref[...]
        copy.wait()

    return pl.pallas_call(
        body,
        out_shape=[shape(*w.shape), shape(*block.shape)],
        in_specs=[hbm(), vmem()],
        out_specs=[vmem(), vmem()],
        scratch_shapes=[pltpu.SemaphoreType.DMA],
        compiler_params=params(),
        cost_estimate=cost(0, 4 << 20),
    )(*outside((w,)), block)


def fetch_behind(weights, after):
    n = len(weights)

    def body(*refs):
        copies = [pltpu.make_async_copy(refs[k], refs[n + 1 + k], refs[-1].at[k]) for k in range(n)]
        for c in copies:
            c.start()
        for c in copies:
            c.wait()

    return pl.pallas_call(
        body,
        out_shape=[shape(*w.shape) for w in weights],
        in_specs=[hbm() for _ in weights] + [pl.BlockSpec(memory_space=pl.ANY)],
        out_specs=[vmem() for _ in weights],
        scratch_shapes=[pltpu.SemaphoreType.DMA((n,))],
        compiler_params=params(),
        cost_estimate=cost(0, 8 << 20),
    )(*outside(weights), after)


def regroup(blocks):
    _, rows, width = blocks[0].shape

    def body(*refs):
        x = [r[0].astype(F32) for r in refs[:-1]]
        low = lax.broadcasted_iota(jnp.int32, (rows, 1), 0) < ROWS
        pairs = list(zip(x[::2], x[1::2]))
        token = [jnp.where(low, a, pltpu.roll(b, ROWS, 0)) for a, b in pairs]
        grads = [jnp.where(low, pltpu.roll(a, ROWS, 0), b) for a, b in pairs]
        refs[-1][0] = jnp.concatenate(token + grads, axis=0).astype(BF16)

    return pl.pallas_call(
        body,
        out_shape=shape(1, rows * len(blocks), width),
        in_specs=[vmem() for _ in blocks],
        out_specs=vmem(),
        compiler_params=params(),
        cost_estimate=cost(0, 64 << 10),
    )(*blocks)


def expert_math(pieces, me, w_gate, w_up, w_down, experts, splits):
    blocks = sum(p.shape[0] for p in pieces)
    width, hid = w_gate.shape
    _, rows, full = pieces[0].shape
    lanes = full - width
    half = rows // 2
    m = blocks * half
    count = len(pieces)

    def body(*refs):
        me_ref, wg_ref, wu_ref, wd_ref = refs[count : count + 4]
        outs = refs[count + 4 :]
        parts, (t_ref, do_ref, h_ref, dg_ref, du_ref) = outs[: len(splits)], outs[len(splits) :]
        x = jnp.concatenate([r[...] for r in refs[:count]], axis=0)
        token = x[:, :half, :width].reshape(m, width)
        t_ref[...] = token
        side = x[:, :half, width:].reshape(m, lanes).astype(F32)
        lane = lax.broadcasted_iota(jnp.int32, (1, lanes), 1)
        mine = me_ref[0]
        scale = jnp.where(lane == mine, 1.0 / 256.0, 0.0) + jnp.where(lane == mine + experts, 1.0 / 65536.0, 0.0)
        coef = jnp.sum(side * scale, axis=1, keepdims=True)
        dout = (coef * x[:, half:, :width].reshape(m, width).astype(F32)).astype(BF16)
        do_ref[...] = dout
        gate = dot(token, wg_ref[...])
        upper = dot(token, wu_ref[...])
        mid = hid // 2
        dact = [dot(wd_ref[:mid], dout, 1, 1).T, dot(dout, wd_ref[mid:], 1, 1)]
        dact = jnp.concatenate(dact, axis=1)
        sig = jax.nn.sigmoid(gate)
        swish = gate * sig
        hidden = (swish * upper).astype(BF16)
        dgate = (dact * upper * sig * (1.0 + gate * (1.0 - sig))).astype(BF16)
        dupper = (dact * swish).astype(BF16)
        h_ref[...], dg_ref[...], du_ref[...] = hidden, dgate, dupper
        part = (coef * dot(hidden, wd_ref[...])).astype(BF16).reshape(blocks, half, width)
        mid = width // 2
        back = (dot(wg_ref[:mid], dgate, 1, 1) + dot(wu_ref[:mid], dupper, 1, 1)).astype(BF16).T
        rest = (dot(dgate, wg_ref[mid:], 1, 1) + dot(dupper, wu_ref[mid:], 1, 1)).astype(BF16)
        back = jnp.concatenate([back, rest], axis=1).reshape(blocks, half, width)
        at = 0
        for ref, n in zip(parts, splits):
            ref[:, :half] = part[at : at + n]
            ref[:, half:] = back[at : at + n]
            at += n

    outs = [shape(n, rows, width) for n in splits]
    outs += [shape(m, width), shape(m, width), shape(m, hid), shape(m, hid), shape(m, hid)]
    got = pl.pallas_call(
        body,
        out_shape=outs,
        in_specs=[vmem()] * count + [pl.BlockSpec(memory_space=pltpu.SMEM)] + [vmem()] * 3,
        out_specs=[vmem() for _ in outs],
        compiler_params=params(LARGE),
        cost_estimate=cost(12 * m * width * hid, 10 << 20),
    )(*pieces, me, w_gate, w_up, w_down)
    return list(got[: len(splits)]), got[len(splits) :]


def weight_grads(left, rights, steps):
    m, rows = left.shape
    cols = rights[0].shape[1]
    steps = steps if rows % (128 * steps) == 0 else 1
    tile = rows // steps

    def body(l_ref, *refs):
        for r_ref, o_ref in zip(refs[: len(rights)], refs[len(rights) :]):
            o_ref[...] = dot(l_ref[...], r_ref[...], 0, 0).astype(BF16)

    return pl.pallas_call(
        body,
        grid=(steps,),
        out_shape=[shape(rows, cols) for _ in rights],
        in_specs=[pl.BlockSpec((m, tile), lambda i: (0, i))] + [pl.BlockSpec((m, cols), lambda i: (0, 0)) for _ in rights],
        out_specs=[pl.BlockSpec((tile, cols), lambda i: (i, 0)) for _ in rights],
        compiler_params=params(LARGE),
        cost_estimate=cost(2 * m * rows * cols * len(rights), 2 * rows * cols * len(rights)),
    )(left, *rights)


def add(terms, splits):
    outs = [shape(n, *terms[0].shape[1:], dtype=BF16 if i else F32) for i, n in enumerate(splits)]

    def body(*refs):
        total = sum(r[...].astype(F32) for r in refs[: len(terms)])
        at = 0
        for ref, n in zip(refs[len(terms) :], splits):
            ref[...] = total[at : at + n].astype(ref.dtype)
            at += n

    return pl.pallas_call(
        body,
        out_shape=outs,
        in_specs=[vmem() for _ in terms],
        out_specs=[vmem() for _ in outs],
        compiler_params=params(),
        cost_estimate=cost(0, 64 << 10),
    )(*terms)


def add_ungroup(terms, after):
    _, rows, width = terms[0].shape
    outs = [shape(1, 2 * ROWS, width, dtype=BF16 if i else F32) for i in range(GROUP)]

    def body(*refs):
        total = sum(r[...].astype(F32) for r in refs[: len(terms)])[0]
        low = lax.broadcasted_iota(jnp.int32, (2 * ROWS, 1), 0) < ROWS
        for i, ref in enumerate(refs[-GROUP:]):
            at = i // 2 * 2 * ROWS
            out, back = total[at : at + 2 * ROWS], total[rows // 2 + at : rows // 2 + at + 2 * ROWS]
            if i % 2:
                block = jnp.where(low, pltpu.roll(out, ROWS, 0), back)
            else:
                block = jnp.where(low, out, pltpu.roll(back, ROWS, 0))
            ref[0] = block.astype(ref.dtype)

    return pl.pallas_call(
        body,
        out_shape=outs,
        in_specs=[vmem() for _ in terms] + [hbm() for _ in after],
        out_specs=[vmem() for _ in outs],
        compiler_params=params(),
        cost_estimate=cost(0, 64 << 10),
    )(*terms, *outside(after))


def add_pair(one, two):
    def body(a_ref, b_ref, o_ref):
        o_ref[...] = (a_ref[...].astype(F32) + b_ref[...].astype(F32)).astype(BF16)

    return pl.pallas_call(
        body,
        out_shape=shape(*one.shape),
        in_specs=[vmem(), vmem()],
        out_specs=vmem(),
        compiler_params=params(),
        cost_estimate=cost(0, 64 << 10),
    )(one, two)


def finish(terms, after=()):
    _, _, width = terms[0].shape

    def body(*refs):
        total = refs[0][...].astype(F32)
        for r in refs[1 : len(terms)]:
            total += r[...].astype(F32)
        out_ref, back_ref = refs[len(terms) + len(after) :]
        out_ref[...] = total[0, :ROWS].astype(BF16)
        back_ref[...] = total[0, ROWS:].astype(BF16)

    return pl.pallas_call(
        body,
        out_shape=[shape(ROWS, width)] * 2,
        in_specs=[vmem() for _ in terms] + [hbm() for _ in after],
        out_specs=[vmem(), vmem()],
        compiler_params=params(),
        cost_estimate=cost(0, 64 << 10),
    )(*terms, *outside(after))


def on_device(tokens, route_ids, route_weights, w_gate, w_up, w_down, grad_out):
    experts = w_gate.shape[0] * lax.axis_size("expert")
    core = lax.axis_size("dp")
    total = lax.axis_size("expert") * core
    plan = stages(total, core)
    me = lax.axis_index("expert").astype(jnp.int32).reshape(1)
    wg, wu, wd = w_gate[0], w_up[0], w_down[0]

    block = pack(tokens, route_ids, route_weights, grad_out, experts)
    block = regroup([block] + exchange_all(block, plan[0], total))
    for masks in plan[1:]:
        held = [block] + exchange_all(block, masks, total)
        block = jnp.concatenate(held, axis=0)
    wg, own = fetch(wg, held[0])
    wu, wd = fetch_behind((wu, wd), held[1])
    pieces = held + [exchange(h, core, total) for h in [own] + held[1:]]

    ways = len(held)
    groups = total // GROUP
    size = groups // 2 // ways
    if groups <= CHUNK:
        parts, kept = expert_math(pieces, me, wg, wu, wd, experts, [size] * (2 * ways))
    else:
        whole = jnp.concatenate(pieces, axis=0)
        sums, saved = [], []
        for at in range(0, groups, CHUNK):
            (got,), rest = expert_math([whole[at : at + CHUNK]], me, wg, wu, wd, experts, [CHUNK])
            sums.append(got)
            saved.append(rest)
        got = jnp.concatenate(sums, axis=0)
        parts = [got[at : at + size] for at in range(0, groups, size)]
        kept = [jnp.concatenate(p, axis=0) for p in zip(*saved)]
    token, dout, hidden, dgate, dupper = kept

    gate_grad, up_grad = weight_grads(token, [dgate, dupper], 2)
    (down_grad,) = weight_grads(hidden, [dout], 2)

    keep, send = parts[:ways], parts[ways:]
    arrived = [exchange(p, core, total) for p in send[::-1]][::-1]
    sums = [add_pair(keep[at], arrived[at]) for at in range(1, ways)]
    terms = [*exchange_all(sums[::-1], plan[-1][::-1], total), keep[0], arrived[0]]
    for masks in reversed(plan[1:-1]):
        ways = len(masks) + 1
        mine, *others = add(terms, [terms[0].shape[0] // ways] * ways)
        terms = [mine, *exchange_all(others[::-1], masks[::-1], total)]
    mine, *others = add_ungroup(terms, (gate_grad,))
    terms = [mine, *exchange_all(others[::-1], plan[0][::-1], total)]
    mixed, back = finish(terms, (down_grad,))
    return mixed, back, gate_grad[None], up_grad[None], down_grad[None]


def solution(mesh):
    rows = P(("groups", "expert", "dp"), None)
    in_specs = (rows, rows, rows, P("expert", None, "dp"), P("expert", None, "dp"), P("expert", "dp", None), rows)
    hidden = P(("groups", "expert"), None, "dp")
    out_specs = (rows, rows, hidden, hidden, P(("groups", "expert"), "dp", None))
    return jax.shard_map(on_device, mesh=mesh, in_specs=in_specs, out_specs=out_specs, check_vma=False)
```

```python
import jax
import jax.numpy as jnp
from jax import lax
from jax.experimental import pallas as pl
from jax.experimental.pallas import tpu as pltpu
from jax.sharding import PartitionSpec as P

AXES = ("expert", "dp")
ROWS = 4
GROUP = 4
CHUNK = 8
LARGE = 16 * 1024 * 1024
SMALL = 4 * 1024 * 1024
F32 = jnp.float32
BF16 = jnp.bfloat16


def vmem():
    return pl.BlockSpec(memory_space=pltpu.VMEM)


def hbm():
    return pl.BlockSpec(memory_space=pltpu.HBM)


def outside(arrays):
    return [pltpu.with_memory_space_constraint(a, pltpu.HBM) for a in arrays]


def shape(*dims, dtype=BF16):
    return jax.ShapeDtypeStruct(dims, dtype)


def params(limit=SMALL):
    return pltpu.CompilerParams(vmem_limit_bytes=limit)


def cost(flops, moved):
    return pl.CostEstimate(flops=flops, bytes_accessed=moved, transcendentals=0)


def dot(a, b, ca=1, cb=0):
    return lax.dot_general(a, b, (((ca,), (cb,)), ((), ())), preferred_element_type=F32)


def exchange(x, mask, total):
    return lax.ppermute(x, AXES, [(i, i ^ mask) for i in range(total)])


def exchange_all(blocks, masks, total):
    if not isinstance(blocks, list):
        blocks = [blocks] * len(masks)
    return [exchange(block, mask, total) for block, mask in zip(blocks, masks)]


def stages(total, core):
    bits = [1 << b for b in reversed(range(total.bit_length() - 1)) if 1 << b != core]
    pairs = [bits[i : i + 2] for i in range(0, len(bits), 2)]
    return [[p[1], p[0], p[0] + p[1]] if len(p) == 2 else p for p in pairs]


def pack(tokens, route_ids, route_weights, grad_out, experts):
    rows, width = tokens.shape
    lanes = -(-2 * experts // 128) * 128

    def body(t_in, i_in, w_in, g_in, o_ref, t_ref, i_ref, w_ref, g_ref, sems):
        pairs = ((t_in, t_ref), (i_in, i_ref), (w_in, w_ref), (g_in, g_ref))
        copies = [pltpu.make_async_copy(a, b, sems.at[k]) for k, (a, b) in enumerate(pairs)]
        for c in copies:
            c.start()
        for c in copies:
            c.wait()
        lane = lax.broadcasted_iota(jnp.int32, (rows, lanes), 1)
        ids, weights = i_ref[...], w_ref[...]
        coded = jnp.zeros((rows, lanes), jnp.int32)
        for k in range(ids.shape[1]):
            one, w = ids[:, k : k + 1], weights[:, k : k + 1]
            coded += jnp.where(lane == one, w >> 8, 0) + jnp.where(lane == one + experts, w & 255, 0)
        both = jnp.concatenate([t_ref[...].astype(F32), g_ref[...].astype(F32)], axis=0)
        side = jnp.concatenate([coded.astype(F32), jnp.zeros((rows, lanes), F32)], axis=0)
        o_ref[0] = jnp.concatenate([both, side], axis=1).astype(BF16)

    args = (tokens, route_ids, route_weights, grad_out)
    return pl.pallas_call(
        body,
        out_shape=shape(1, 2 * rows, width + lanes),
        in_specs=[hbm() for _ in args],
        out_specs=vmem(),
        scratch_shapes=[pltpu.VMEM(a.shape, a.dtype) for a in args] + [pltpu.SemaphoreType.DMA((len(args),))],
        compiler_params=params(),
        cost_estimate=cost(0, 80 << 10),
    )(*outside(args))


def fetch(w, block):
    def body(w_ref, b_ref, o_ref, c_ref, sem):
        copy = pltpu.make_async_copy(w_ref, o_ref, sem)
        copy.start()
        c_ref[...] = b_ref[...]
        copy.wait()

    return pl.pallas_call(
        body,
        out_shape=[shape(*w.shape), shape(*block.shape)],
        in_specs=[hbm(), vmem()],
        out_specs=[vmem(), vmem()],
        scratch_shapes=[pltpu.SemaphoreType.DMA],
        compiler_params=params(),
        cost_estimate=cost(0, 4 << 20),
    )(*outside((w,)), block)


def fetch_behind(weights, inside, after):
    n = len(weights)

    def body(*refs):
        outs = refs[n + 2 : -1]
        copies = [pltpu.make_async_copy(refs[k], outs[k], refs[-1].at[k]) for k in range(n)]
        for c in copies:
            c.start()
        outs[n][...] = refs[n][...].T
        copies[0].wait()
        outs[n + 1][...] = outs[0][...].T
        for c in copies[1:]:
            c.wait()

    return pl.pallas_call(
        body,
        out_shape=[shape(*w.shape) for w in weights] + [shape(*inside.shape[::-1]), shape(*weights[0].shape[::-1])],
        in_specs=[hbm() for _ in weights] + [vmem(), pl.BlockSpec(memory_space=pl.ANY)],
        out_specs=[vmem() for _ in range(n + 2)],
        scratch_shapes=[pltpu.SemaphoreType.DMA((n,))],
        compiler_params=params(),
        cost_estimate=cost(0, 8 << 20),
    )(*outside(weights), inside, after)


def regroup(blocks):
    _, rows, width = blocks[0].shape

    def body(*refs):
        x = [r[0].astype(F32) for r in refs[:-1]]
        low = lax.broadcasted_iota(jnp.int32, (rows, 1), 0) < ROWS
        pairs = list(zip(x[::2], x[1::2]))
        token = [jnp.where(low, a, pltpu.roll(b, ROWS, 0)) for a, b in pairs]
        grads = [jnp.where(low, pltpu.roll(a, ROWS, 0), b) for a, b in pairs]
        refs[-1][0] = jnp.concatenate(token + grads, axis=0).astype(BF16)

    return pl.pallas_call(
        body,
        out_shape=shape(1, rows * len(blocks), width),
        in_specs=[vmem() for _ in blocks],
        out_specs=vmem(),
        compiler_params=params(),
        cost_estimate=cost(0, 64 << 10),
    )(*blocks)


def expert_math(pieces, me, w_gate, turned, w_up, w_down, experts, splits):
    blocks = sum(p.shape[0] for p in pieces)
    width, hid = w_gate.shape
    _, rows, full = pieces[0].shape
    lanes = full - width
    half = rows // 2
    m = blocks * half
    count = len(pieces)

    def body(*refs):
        me_ref, wg_ref, gw_ref, dw_ref, wu_ref, wd_ref = refs[count : count + 6]
        outs = refs[count + 6 :]
        parts, (t_ref, do_ref, h_ref, dg_ref, du_ref) = outs[: len(splits)], outs[len(splits) :]
        x = jnp.concatenate([r[...] for r in refs[:count]], axis=0)
        token = x[:, :half, :width].reshape(m, width)
        t_ref[...] = token
        side = x[:, :half, width:].reshape(m, lanes).astype(F32)
        lane = lax.broadcasted_iota(jnp.int32, (1, lanes), 1)
        mine = me_ref[0]
        scale = jnp.where(lane == mine, 1.0 / 256.0, 0.0) + jnp.where(lane == mine + experts, 1.0 / 65536.0, 0.0)
        coef = jnp.sum(side * scale, axis=1, keepdims=True)
        dout = (coef * x[:, half:, :width].reshape(m, width).astype(F32)).astype(BF16)
        do_ref[...] = dout
        gate = dot(token, wg_ref[...])
        upper = dot(token, wu_ref[...])
        dact = dot(dout, dw_ref[...])
        sig = jax.nn.sigmoid(gate)
        swish = gate * sig
        hidden = (swish * upper).astype(BF16)
        dgate = (dact * upper * sig * (1.0 + gate * (1.0 - sig))).astype(BF16)
        dupper = (dact * swish).astype(BF16)
        h_ref[...], dg_ref[...], du_ref[...] = hidden, dgate, dupper
        part = (coef * dot(hidden, wd_ref[...])).astype(BF16).reshape(blocks, half, width)
        mid = width // 2
        back = [dot(wu_ref[:mid], dupper, 1, 1).T, dot(dupper, wu_ref[mid:], 1, 1)]
        back = dot(dgate, gw_ref[...]) + jnp.concatenate(back, axis=1)
        back = back.astype(BF16).reshape(blocks, half, width)
        at = 0
        for ref, n in zip(parts, splits):
            ref[:, :half] = part[at : at + n]
            ref[:, half:] = back[at : at + n]
            at += n

    outs = [shape(n, rows, width) for n in splits]
    outs += [shape(m, width), shape(m, width), shape(m, hid), shape(m, hid), shape(m, hid)]
    got = pl.pallas_call(
        body,
        out_shape=outs,
        in_specs=[vmem()] * count + [pl.BlockSpec(memory_space=pltpu.SMEM)] + [vmem()] * 5,
        out_specs=[vmem() for _ in outs],
        compiler_params=params(LARGE),
        cost_estimate=cost(12 * m * width * hid, 10 << 20),
    )(*pieces, me, w_gate, *turned, w_up, w_down)
    return list(got[: len(splits)]), got[len(splits) :]


def weight_grads(left, rights, steps):
    m, rows = left.shape
    cols = rights[0].shape[1]
    steps = steps if rows % (128 * steps) == 0 else 1
    tile = rows // steps

    def body(l_ref, *refs):
        for r_ref, o_ref in zip(refs[: len(rights)], refs[len(rights) :]):
            o_ref[...] = dot(l_ref[...], r_ref[...], 0, 0).astype(BF16)

    return pl.pallas_call(
        body,
        grid=(steps,),
        out_shape=[shape(rows, cols) for _ in rights],
        in_specs=[pl.BlockSpec((m, tile), lambda i: (0, i))] + [pl.BlockSpec((m, cols), lambda i: (0, 0)) for _ in rights],
        out_specs=[pl.BlockSpec((tile, cols), lambda i: (i, 0)) for _ in rights],
        compiler_params=params(LARGE),
        cost_estimate=cost(2 * m * rows * cols * len(rights), 2 * rows * cols * len(rights)),
    )(left, *rights)


def add(terms, splits):
    outs = [shape(n, *terms[0].shape[1:], dtype=BF16 if i else F32) for i, n in enumerate(splits)]

    def body(*refs):
        total = sum(r[...].astype(F32) for r in refs[: len(terms)])
        at = 0
        for ref, n in zip(refs[len(terms) :], splits):
            ref[...] = total[at : at + n].astype(ref.dtype)
            at += n

    return pl.pallas_call(
        body,
        out_shape=outs,
        in_specs=[vmem() for _ in terms],
        out_specs=[vmem() for _ in outs],
        compiler_params=params(),
        cost_estimate=cost(0, 64 << 10),
    )(*terms)


def add_ungroup(terms, after):
    _, rows, width = terms[0].shape
    outs = [shape(1, 2 * ROWS, width, dtype=BF16 if i else F32) for i in range(GROUP)]

    def body(*refs):
        total = sum(r[...].astype(F32) for r in refs[: len(terms)])[0]
        low = lax.broadcasted_iota(jnp.int32, (2 * ROWS, 1), 0) < ROWS
        for i, ref in enumerate(refs[-GROUP:]):
            at = i // 2 * 2 * ROWS
            out, back = total[at : at + 2 * ROWS], total[rows // 2 + at : rows // 2 + at + 2 * ROWS]
            if i % 2:
                block = jnp.where(low, pltpu.roll(out, ROWS, 0), back)
            else:
                block = jnp.where(low, out, pltpu.roll(back, ROWS, 0))
            ref[0] = block.astype(ref.dtype)

    return pl.pallas_call(
        body,
        out_shape=outs,
        in_specs=[vmem() for _ in terms] + [hbm() for _ in after],
        out_specs=[vmem() for _ in outs],
        compiler_params=params(),
        cost_estimate=cost(0, 64 << 10),
    )(*terms, *outside(after))


def add_pair(one, two):
    def body(a_ref, b_ref, o_ref):
        o_ref[...] = (a_ref[...].astype(F32) + b_ref[...].astype(F32)).astype(BF16)

    return pl.pallas_call(
        body,
        out_shape=shape(*one.shape),
        in_specs=[vmem(), vmem()],
        out_specs=vmem(),
        compiler_params=params(),
        cost_estimate=cost(0, 64 << 10),
    )(one, two)


def finish(terms, after=()):
    _, _, width = terms[0].shape

    def body(*refs):
        total = refs[0][...].astype(F32)
        for r in refs[1 : len(terms)]:
            total += r[...].astype(F32)
        out_ref, back_ref = refs[len(terms) + len(after) :]
        out_ref[...] = total[0, :ROWS].astype(BF16)
        back_ref[...] = total[0, ROWS:].astype(BF16)

    return pl.pallas_call(
        body,
        out_shape=[shape(ROWS, width)] * 2,
        in_specs=[vmem() for _ in terms] + [hbm() for _ in after],
        out_specs=[vmem(), vmem()],
        compiler_params=params(),
        cost_estimate=cost(0, 64 << 10),
    )(*terms, *outside(after))


def on_device(tokens, route_ids, route_weights, w_gate, w_up, w_down, grad_out):
    experts = w_gate.shape[0] * lax.axis_size("expert")
    core = lax.axis_size("dp")
    total = lax.axis_size("expert") * core
    plan = stages(total, core)
    me = lax.axis_index("expert").astype(jnp.int32).reshape(1)
    wg, wu, wd = w_gate[0], w_up[0], w_down[0]

    block = pack(tokens, route_ids, route_weights, grad_out, experts)
    block = regroup([block] + exchange_all(block, plan[0], total))
    for masks in plan[1:]:
        held = [block] + exchange_all(block, masks, total)
        block = jnp.concatenate(held, axis=0)
    wg, own = fetch(wg, held[0])
    wd, wu, *turned = fetch_behind((wd, wu), wg, held[1])
    pieces = held + [exchange(h, core, total) for h in [own] + held[1:]]

    ways = len(held)
    groups = total // GROUP
    size = groups // 2 // ways
    if groups <= CHUNK:
        parts, kept = expert_math(pieces, me, wg, turned, wu, wd, experts, [size] * (2 * ways))
    else:
        whole = jnp.concatenate(pieces, axis=0)
        sums, saved = [], []
        for at in range(0, groups, CHUNK):
            (got,), rest = expert_math([whole[at : at + CHUNK]], me, wg, turned, wu, wd, experts, [CHUNK])
            sums.append(got)
            saved.append(rest)
        got = jnp.concatenate(sums, axis=0)
        parts = [got[at : at + size] for at in range(0, groups, size)]
        kept = [jnp.concatenate(p, axis=0) for p in zip(*saved)]
    token, dout, hidden, dgate, dupper = kept

    gate_grad, up_grad = weight_grads(token, [dgate, dupper], 2)
    (down_grad,) = weight_grads(hidden, [dout], 2)

    keep, send = parts[:ways], parts[ways:]
    arrived = [exchange(p, core, total) for p in send[::-1]][::-1]
    sums = [add_pair(keep[at], arrived[at]) for at in range(1, ways)]
    terms = [*exchange_all(sums[::-1], plan[-1][::-1], total), keep[0], arrived[0]]
    for masks in reversed(plan[1:-1]):
        ways = len(masks) + 1
        mine, *others = add(terms, [terms[0].shape[0] // ways] * ways)
        terms = [mine, *exchange_all(others[::-1], masks[::-1], total)]
    mine, *others = add_ungroup(terms, (gate_grad,))
    terms = [mine, *exchange_all(others[::-1], plan[0][::-1], total)]
    mixed, back = finish(terms, (down_grad,))
    return mixed, back, gate_grad[None], up_grad[None], down_grad[None]


def solution(mesh):
    rows = P(("groups", "expert", "dp"), None)
    in_specs = (rows, rows, rows, P("expert", None, "dp"), P("expert", None, "dp"), P("expert", "dp", None), rows)
    hidden = P(("groups", "expert"), None, "dp")
    out_specs = (rows, rows, hidden, hidden, P(("groups", "expert"), "dp", None))
    return jax.shard_map(on_device, mesh=mesh, in_specs=in_specs, out_specs=out_specs, check_vma=False)
```

```python
import jax
import jax.numpy as jnp
from jax import lax
from jax.experimental import pallas as pl
from jax.experimental.pallas import tpu as pltpu
from jax.sharding import PartitionSpec as P

AXES = ("expert", "dp")
ROWS = 4
GROUP = 4
CHUNK = 8
LARGE = 16 * 1024 * 1024
SMALL = 4 * 1024 * 1024
F32 = jnp.float32
BF16 = jnp.bfloat16


def vmem():
    return pl.BlockSpec(memory_space=pltpu.VMEM)


def hbm():
    return pl.BlockSpec(memory_space=pltpu.HBM)


def outside(arrays):
    return [pltpu.with_memory_space_constraint(a, pltpu.HBM) for a in arrays]


def shape(*dims, dtype=BF16):
    return jax.ShapeDtypeStruct(dims, dtype)


def params(limit=SMALL):
    return pltpu.CompilerParams(vmem_limit_bytes=limit)


def cost(flops, moved):
    return pl.CostEstimate(flops=flops, bytes_accessed=moved, transcendentals=0)


def dot(a, b, ca=1, cb=0):
    return lax.dot_general(a, b, (((ca,), (cb,)), ((), ())), preferred_element_type=F32)


def exchange(x, mask, total):
    return lax.ppermute(x, AXES, [(i, i ^ mask) for i in range(total)])


def exchange_all(blocks, masks, total):
    if not isinstance(blocks, list):
        blocks = [blocks] * len(masks)
    return [exchange(block, mask, total) for block, mask in zip(blocks, masks)]


def stages(total, core):
    bits = [1 << b for b in reversed(range(total.bit_length() - 1)) if 1 << b != core]
    pairs = [bits[i : i + 2] for i in range(0, len(bits), 2)]
    return [[p[1], p[0], p[0] + p[1]] if len(p) == 2 else p for p in pairs]


def pack(tokens, route_ids, route_weights, grad_out, experts):
    rows, width = tokens.shape
    lanes = -(-2 * experts // 128) * 128

    def body(t_in, i_in, w_in, g_in, o_ref, t_ref, i_ref, w_ref, g_ref, sems):
        pairs = ((t_in, t_ref), (i_in, i_ref), (w_in, w_ref), (g_in, g_ref))
        copies = [pltpu.make_async_copy(a, b, sems.at[k]) for k, (a, b) in enumerate(pairs)]
        for c in copies:
            c.start()
        for c in copies:
            c.wait()
        lane = lax.broadcasted_iota(jnp.int32, (rows, lanes), 1)
        ids, weights = i_ref[...], w_ref[...]
        coded = jnp.zeros((rows, lanes), jnp.int32)
        for k in range(ids.shape[1]):
            one, w = ids[:, k : k + 1], weights[:, k : k + 1]
            coded += jnp.where(lane == one, w >> 8, 0) + jnp.where(lane == one + experts, w & 255, 0)
        both = jnp.concatenate([t_ref[...].astype(F32), g_ref[...].astype(F32)], axis=0)
        side = jnp.concatenate([coded.astype(F32), jnp.zeros((rows, lanes), F32)], axis=0)
        o_ref[0] = jnp.concatenate([both, side], axis=1).astype(BF16)

    args = (tokens, route_ids, route_weights, grad_out)
    return pl.pallas_call(
        body,
        out_shape=shape(1, 2 * rows, width + lanes),
        in_specs=[hbm() for _ in args],
        out_specs=vmem(),
        scratch_shapes=[pltpu.VMEM(a.shape, a.dtype) for a in args] + [pltpu.SemaphoreType.DMA((len(args),))],
        compiler_params=params(),
        cost_estimate=cost(0, 80 << 10),
    )(*outside(args))


def fetch(w, block):
    def body(w_ref, b_ref, o_ref, c_ref, sem):
        copy = pltpu.make_async_copy(w_ref, o_ref, sem)
        copy.start()
        c_ref[...] = b_ref[...]
        copy.wait()

    return pl.pallas_call(
        body,
        out_shape=[shape(*w.shape), shape(*block.shape)],
        in_specs=[hbm(), vmem()],
        out_specs=[vmem(), vmem()],
        scratch_shapes=[pltpu.SemaphoreType.DMA],
        compiler_params=params(),
        cost_estimate=cost(0, 4 << 20),
    )(*outside((w,)), block)


def rows_of(x, width, mine, experts):
    blocks, rows, full = x.shape
    half, lanes = rows // 2, full - width
    m = blocks * half
    token = x[:, :half, :width].reshape(m, width)
    side = x[:, :half, width:].reshape(m, lanes).astype(F32)
    lane = lax.broadcasted_iota(jnp.int32, (1, lanes), 1)
    scale = jnp.where(lane == mine, 1.0 / 256.0, 0.0) + jnp.where(lane == mine + experts, 1.0 / 65536.0, 0.0)
    coef = jnp.sum(side * scale, axis=1, keepdims=True)
    return token, coef, (coef * x[:, half:, :width].reshape(m, width).astype(F32)).astype(BF16)


def fetch_behind(weights, inside, held, me, experts):
    n = len(weights)
    count = len(held)
    width = inside.shape[0]
    m = sum(h.shape[0] * h.shape[1] for h in held) // 2

    def body(*refs):
        outs = refs[n + 2 + count : -1]
        copies = [pltpu.make_async_copy(refs[k], outs[k], refs[-1].at[k]) for k in range(n)]
        for c in copies:
            c.start()
        outs[n][...] = refs[n][...].T
        x = jnp.concatenate([r[...] for r in refs[n + 2 : n + 2 + count]], axis=0)
        token, coef, dout = rows_of(x, width, refs[n + 1][0], experts)
        outs[n + 2][...], outs[n + 4][...] = token, dout
        outs[n + 3][...] = jnp.broadcast_to(coef, (m, 128))
        copies[0].wait()
        outs[n + 1][...] = outs[0][...].T
        for c in copies[1:]:
            c.wait()

    return pl.pallas_call(
        body,
        out_shape=[shape(*w.shape) for w in weights] + [shape(*inside.shape[::-1]), shape(*weights[0].shape[::-1])]
        + [shape(m, width), shape(m, 128, dtype=F32), shape(m, width)],
        in_specs=[hbm() for _ in weights] + [vmem(), pl.BlockSpec(memory_space=pltpu.SMEM)] + [vmem()] * count,
        out_specs=[vmem() for _ in range(n + 5)],
        scratch_shapes=[pltpu.SemaphoreType.DMA((n,))],
        compiler_params=params(LARGE),
        cost_estimate=cost(0, 8 << 20),
    )(*outside(weights), inside, me, *held)


def regroup(blocks):
    _, rows, width = blocks[0].shape

    def body(*refs):
        x = [r[0].astype(F32) for r in refs[:-1]]
        low = lax.broadcasted_iota(jnp.int32, (rows, 1), 0) < ROWS
        pairs = list(zip(x[::2], x[1::2]))
        token = [jnp.where(low, a, pltpu.roll(b, ROWS, 0)) for a, b in pairs]
        grads = [jnp.where(low, pltpu.roll(a, ROWS, 0), b) for a, b in pairs]
        refs[-1][0] = jnp.concatenate(token + grads, axis=0).astype(BF16)

    return pl.pallas_call(
        body,
        out_shape=shape(1, rows * len(blocks), width),
        in_specs=[vmem() for _ in blocks],
        out_specs=vmem(),
        compiler_params=params(),
        cost_estimate=cost(0, 64 << 10),
    )(*blocks)


def expert_math(pieces, ready, me, w_gate, turned, w_up, w_down, experts, splits):
    blocks = sum(splits)
    width, hid = w_gate.shape
    _, rows, full = pieces[0].shape
    half = rows // 2
    m = blocks * half
    count, had = len(pieces), len(ready)

    def body(*refs):
        early, refs = refs[count : count + had], refs[:count] + refs[count + had :]
        me_ref, wg_ref, gw_ref, dw_ref, wu_ref, wd_ref = refs[count : count + 6]
        outs = refs[count + 6 :]
        parts, (t_ref, do_ref, h_ref, dg_ref, du_ref) = outs[: len(splits)], outs[len(splits) :]
        x = jnp.concatenate([r[...] for r in refs[:count]], axis=0)
        token, coef, dout = rows_of(x, width, me_ref[0], experts)
        if had:
            token = jnp.concatenate([early[0][...], token], axis=0)
            coef = jnp.concatenate([early[1][:, :1], coef], axis=0)
            dout = jnp.concatenate([early[2][...], dout], axis=0)
        t_ref[...], do_ref[...] = token, dout
        gate = dot(token, wg_ref[...])
        upper = dot(token, wu_ref[...])
        dact = dot(dout, dw_ref[...])
        sig = jax.nn.sigmoid(gate)
        swish = gate * sig
        hidden = (swish * upper).astype(BF16)
        dgate = (dact * upper * sig * (1.0 + gate * (1.0 - sig))).astype(BF16)
        dupper = (dact * swish).astype(BF16)
        h_ref[...], dg_ref[...], du_ref[...] = hidden, dgate, dupper
        part = (coef * dot(hidden, wd_ref[...])).astype(BF16).reshape(blocks, half, width)
        mid = width // 2
        back = [dot(wu_ref[:mid], dupper, 1, 1).T, dot(dupper, wu_ref[mid:], 1, 1)]
        back = dot(dgate, gw_ref[...]) + jnp.concatenate(back, axis=1)
        back = back.astype(BF16).reshape(blocks, half, width)
        at = 0
        for ref, n in zip(parts, splits):
            ref[:, :half] = part[at : at + n]
            ref[:, half:] = back[at : at + n]
            at += n

    outs = [shape(n, rows, width) for n in splits]
    outs += [shape(m, width), shape(m, width), shape(m, hid), shape(m, hid), shape(m, hid)]
    got = pl.pallas_call(
        body,
        out_shape=outs,
        in_specs=[vmem()] * (count + had) + [pl.BlockSpec(memory_space=pltpu.SMEM)] + [vmem()] * 5,
        out_specs=[vmem() for _ in outs],
        compiler_params=params(LARGE),
        cost_estimate=cost(12 * m * width * hid, 10 << 20),
    )(*pieces, *ready, me, w_gate, *turned, w_up, w_down)
    return list(got[: len(splits)]), got[len(splits) :]


def weight_grads(left, rights, steps):
    m, rows = left.shape
    cols = rights[0].shape[1]
    steps = steps if rows % (128 * steps) == 0 else 1
    tile = rows // steps

    def body(l_ref, *refs):
        for r_ref, o_ref in zip(refs[: len(rights)], refs[len(rights) :]):
            o_ref[...] = dot(l_ref[...], r_ref[...], 0, 0).astype(BF16)

    return pl.pallas_call(
        body,
        grid=(steps,),
        out_shape=[shape(rows, cols) for _ in rights],
        in_specs=[pl.BlockSpec((m, tile), lambda i: (0, i))] + [pl.BlockSpec((m, cols), lambda i: (0, 0)) for _ in rights],
        out_specs=[pl.BlockSpec((tile, cols), lambda i: (i, 0)) for _ in rights],
        compiler_params=params(LARGE),
        cost_estimate=cost(2 * m * rows * cols * len(rights), 2 * rows * cols * len(rights)),
    )(left, *rights)


def add(terms, splits):
    outs = [shape(n, *terms[0].shape[1:], dtype=BF16 if i else F32) for i, n in enumerate(splits)]

    def body(*refs):
        total = sum(r[...].astype(F32) for r in refs[: len(terms)])
        at = 0
        for ref, n in zip(refs[len(terms) :], splits):
            ref[...] = total[at : at + n].astype(ref.dtype)
            at += n

    return pl.pallas_call(
        body,
        out_shape=outs,
        in_specs=[vmem() for _ in terms],
        out_specs=[vmem() for _ in outs],
        compiler_params=params(),
        cost_estimate=cost(0, 64 << 10),
    )(*terms)


def add_ungroup(terms, after):
    _, rows, width = terms[0].shape
    outs = [shape(1, 2 * ROWS, width, dtype=BF16 if i else F32) for i in range(GROUP)]

    def body(*refs):
        total = sum(r[...].astype(F32) for r in refs[: len(terms)])[0]
        low = lax.broadcasted_iota(jnp.int32, (2 * ROWS, 1), 0) < ROWS
        for i, ref in enumerate(refs[-GROUP:]):
            at = i // 2 * 2 * ROWS
            out, back = total[at : at + 2 * ROWS], total[rows // 2 + at : rows // 2 + at + 2 * ROWS]
            if i % 2:
                block = jnp.where(low, pltpu.roll(out, ROWS, 0), back)
            else:
                block = jnp.where(low, out, pltpu.roll(back, ROWS, 0))
            ref[0] = block.astype(ref.dtype)

    return pl.pallas_call(
        body,
        out_shape=outs,
        in_specs=[vmem() for _ in terms] + [hbm() for _ in after],
        out_specs=[vmem() for _ in outs],
        compiler_params=params(),
        cost_estimate=cost(0, 64 << 10),
    )(*terms, *outside(after))


def add_pair(one, two):
    def body(a_ref, b_ref, o_ref):
        o_ref[...] = (a_ref[...].astype(F32) + b_ref[...].astype(F32)).astype(BF16)

    return pl.pallas_call(
        body,
        out_shape=shape(*one.shape),
        in_specs=[vmem(), vmem()],
        out_specs=vmem(),
        compiler_params=params(),
        cost_estimate=cost(0, 64 << 10),
    )(one, two)


def finish(terms, after=()):
    _, _, width = terms[0].shape

    def body(*refs):
        total = refs[0][...].astype(F32)
        for r in refs[1 : len(terms)]:
            total += r[...].astype(F32)
        out_ref, back_ref = refs[len(terms) + len(after) :]
        out_ref[...] = total[0, :ROWS].astype(BF16)
        back_ref[...] = total[0, ROWS:].astype(BF16)

    return pl.pallas_call(
        body,
        out_shape=[shape(ROWS, width)] * 2,
        in_specs=[vmem() for _ in terms] + [hbm() for _ in after],
        out_specs=[vmem(), vmem()],
        compiler_params=params(),
        cost_estimate=cost(0, 64 << 10),
    )(*terms, *outside(after))


def on_device(tokens, route_ids, route_weights, w_gate, w_up, w_down, grad_out):
    experts = w_gate.shape[0] * lax.axis_size("expert")
    core = lax.axis_size("dp")
    total = lax.axis_size("expert") * core
    plan = stages(total, core)
    me = lax.axis_index("expert").astype(jnp.int32).reshape(1)
    wg, wu, wd = w_gate[0], w_up[0], w_down[0]

    block = pack(tokens, route_ids, route_weights, grad_out, experts)
    block = regroup([block] + exchange_all(block, plan[0], total))
    for masks in plan[1:]:
        held = [block] + exchange_all(block, masks, total)
        block = jnp.concatenate(held, axis=0)
    wg, own = fetch(wg, held[0])
    wd, wu, *turned = fetch_behind((wd, wu), wg, held, me, experts)
    turned, ready = turned[:2], turned[2:]
    pieces = held + [exchange(h, core, total) for h in [own] + held[1:]]

    ways = len(held)
    groups = total // GROUP
    size = groups // 2 // ways
    if groups <= CHUNK:
        parts, kept = expert_math(pieces[len(held) :], ready, me, wg, turned, wu, wd, experts, [size] * (2 * ways))
    else:
        whole = jnp.concatenate(pieces, axis=0)
        sums, saved = [], []
        for at in range(0, groups, CHUNK):
            (got,), rest = expert_math([whole[at : at + CHUNK]], [], me, wg, turned, wu, wd, experts, [CHUNK])
            sums.append(got)
            saved.append(rest)
        got = jnp.concatenate(sums, axis=0)
        parts = [got[at : at + size] for at in range(0, groups, size)]
        kept = [jnp.concatenate(p, axis=0) for p in zip(*saved)]
    token, dout, hidden, dgate, dupper = kept

    gate_grad, up_grad = weight_grads(token, [dgate, dupper], 2)
    (down_grad,) = weight_grads(hidden, [dout], 2)

    keep, send = parts[:ways], parts[ways:]
    arrived = [exchange(p, core, total) for p in send[::-1]][::-1]
    sums = [add_pair(keep[at], arrived[at]) for at in range(1, ways)]
    terms = [*exchange_all(sums[::-1], plan[-1][::-1], total), keep[0], arrived[0]]
    for masks in reversed(plan[1:-1]):
        ways = len(masks) + 1
        mine, *others = add(terms, [terms[0].shape[0] // ways] * ways)
        terms = [mine, *exchange_all(others[::-1], masks[::-1], total)]
    mine, *others = add_ungroup(terms, (gate_grad,))
    terms = [mine, *exchange_all(others[::-1], plan[0][::-1], total)]
    mixed, back = finish(terms, (down_grad,))
    return mixed, back, gate_grad[None], up_grad[None], down_grad[None]


def solution(mesh):
    rows = P(("groups", "expert", "dp"), None)
    in_specs = (rows, rows, rows, P("expert", None, "dp"), P("expert", None, "dp"), P("expert", "dp", None), rows)
    hidden = P(("groups", "expert"), None, "dp")
    out_specs = (rows, rows, hidden, hidden, P(("groups", "expert"), "dp", None))
    return jax.shard_map(on_device, mesh=mesh, in_specs=in_specs, out_specs=out_specs, check_vma=False)
```

```python
import jax
import jax.numpy as jnp
from jax import lax
from jax.experimental import pallas as pl
from jax.experimental.pallas import tpu as pltpu
from jax.sharding import PartitionSpec as P

AXES = ("expert", "dp")
ROWS = 4
GROUP = 4
CHUNK = 8
LARGE = 16 * 1024 * 1024
SMALL = 4 * 1024 * 1024
F32 = jnp.float32
BF16 = jnp.bfloat16


def vmem():
    return pl.BlockSpec(memory_space=pltpu.VMEM)


def hbm():
    return pl.BlockSpec(memory_space=pltpu.HBM)


def outside(arrays):
    return [pltpu.with_memory_space_constraint(a, pltpu.HBM) for a in arrays]


def shape(*dims, dtype=BF16):
    return jax.ShapeDtypeStruct(dims, dtype)


def params(limit=SMALL):
    return pltpu.CompilerParams(vmem_limit_bytes=limit)


def cost(flops, moved):
    return pl.CostEstimate(flops=flops, bytes_accessed=moved, transcendentals=0)


def dot(a, b, ca=1, cb=0):
    return lax.dot_general(a, b, (((ca,), (cb,)), ((), ())), preferred_element_type=F32)


def exchange(x, mask, total):
    return lax.ppermute(x, AXES, [(i, i ^ mask) for i in range(total)])


def exchange_all(blocks, masks, total):
    if not isinstance(blocks, list):
        blocks = [blocks] * len(masks)
    return [exchange(block, mask, total) for block, mask in zip(blocks, masks)]


def stages(total, core):
    bits = [1 << b for b in reversed(range(total.bit_length() - 1)) if 1 << b != core]
    pairs = [bits[i : i + 2] for i in range(0, len(bits), 2)]
    return [[p[1], p[0], p[0] + p[1]] if len(p) == 2 else p for p in pairs]


def pack(tokens, route_ids, route_weights, grad_out, experts):
    rows, width = tokens.shape
    lanes = -(-2 * experts // 128) * 128

    def body(t_in, i_in, w_in, g_in, o_ref, t_ref, i_ref, w_ref, g_ref, sems):
        pairs = ((t_in, t_ref), (i_in, i_ref), (w_in, w_ref), (g_in, g_ref))
        copies = [pltpu.make_async_copy(a, b, sems.at[k]) for k, (a, b) in enumerate(pairs)]
        for c in copies:
            c.start()
        for c in copies:
            c.wait()
        lane = lax.broadcasted_iota(jnp.int32, (rows, lanes), 1)
        ids, weights = i_ref[...], w_ref[...]
        coded = jnp.zeros((rows, lanes), jnp.int32)
        for k in range(ids.shape[1]):
            one, w = ids[:, k : k + 1], weights[:, k : k + 1]
            coded += jnp.where(lane == one, w >> 8, 0) + jnp.where(lane == one + experts, w & 255, 0)
        both = jnp.concatenate([t_ref[...].astype(F32), g_ref[...].astype(F32)], axis=0)
        side = jnp.concatenate([coded.astype(F32), jnp.zeros((rows, lanes), F32)], axis=0)
        o_ref[0] = jnp.concatenate([both, side], axis=1).astype(BF16)

    args = (tokens, route_ids, route_weights, grad_out)
    return pl.pallas_call(
        body,
        out_shape=shape(1, 2 * rows, width + lanes),
        in_specs=[hbm() for _ in args],
        out_specs=vmem(),
        scratch_shapes=[pltpu.VMEM(a.shape, a.dtype) for a in args] + [pltpu.SemaphoreType.DMA((len(args),))],
        compiler_params=params(),
        cost_estimate=cost(0, 80 << 10),
    )(*outside(args))


def fetch(w, block):
    def body(w_ref, b_ref, o_ref, c_ref, sem):
        copy = pltpu.make_async_copy(w_ref, o_ref, sem)
        copy.start()
        c_ref[...] = b_ref[...]
        copy.wait()

    return pl.pallas_call(
        body,
        out_shape=[shape(*w.shape), shape(*block.shape)],
        in_specs=[hbm(), vmem()],
        out_specs=[vmem(), vmem()],
        scratch_shapes=[pltpu.SemaphoreType.DMA],
        compiler_params=params(),
        cost_estimate=cost(0, 4 << 20),
    )(*outside((w,)), block)


def rows_of(x, width, mine, experts):
    blocks, rows, full = x.shape
    half, lanes = rows // 2, full - width
    m = blocks * half
    token = x[:, :half, :width].reshape(m, width)
    side = x[:, :half, width:].reshape(m, lanes).astype(F32)
    lane = lax.broadcasted_iota(jnp.int32, (1, lanes), 1)
    scale = jnp.where(lane == mine, 1.0 / 256.0, 0.0) + jnp.where(lane == mine + experts, 1.0 / 65536.0, 0.0)
    coef = jnp.sum(side * scale, axis=1, keepdims=True)
    return token, coef, (coef * x[:, half:, :width].reshape(m, width).astype(F32)).astype(BF16)


def fetch_behind(weights, inside, held, me, experts):
    n = len(weights)
    count = len(held)
    width = inside.shape[0]
    m = sum(h.shape[0] * h.shape[1] for h in held) // 2

    def body(*refs):
        outs = refs[n + 2 + count : -1]
        copies = [pltpu.make_async_copy(refs[k], outs[k], refs[-1].at[k]) for k in range(n)]
        for c in copies:
            c.start()
        outs[n][...] = refs[n][...].T
        x = jnp.concatenate([r[...] for r in refs[n + 2 : n + 2 + count]], axis=0)
        token, coef, dout = rows_of(x, width, refs[n + 1][0], experts)
        outs[n + 2][...], outs[n + 4][...] = token, dout
        outs[n + 3][...] = jnp.broadcast_to(coef, (m, 128))
        copies[0].wait()
        outs[n + 1][...] = outs[0][...].T
        for c in copies[1:]:
            c.wait()

    return pl.pallas_call(
        body,
        out_shape=[shape(*w.shape) for w in weights] + [shape(*inside.shape[::-1]), shape(*weights[0].shape[::-1])]
        + [shape(m, width), shape(m, 128, dtype=F32), shape(m, width)],
        in_specs=[hbm() for _ in weights] + [vmem(), pl.BlockSpec(memory_space=pltpu.SMEM)] + [vmem()] * count,
        out_specs=[vmem() for _ in range(n + 5)],
        scratch_shapes=[pltpu.SemaphoreType.DMA((n,))],
        compiler_params=params(LARGE),
        cost_estimate=cost(0, 8 << 20),
    )(*outside(weights), inside, me, *held)


def regroup(blocks):
    _, rows, width = blocks[0].shape

    def body(*refs):
        x = [r[0].astype(F32) for r in refs[:-1]]
        low = lax.broadcasted_iota(jnp.int32, (rows, 1), 0) < ROWS
        pairs = list(zip(x[::2], x[1::2]))
        token = [jnp.where(low, a, pltpu.roll(b, ROWS, 0)) for a, b in pairs]
        grads = [jnp.where(low, pltpu.roll(a, ROWS, 0), b) for a, b in pairs]
        refs[-1][0] = jnp.concatenate(token + grads, axis=0).astype(BF16)

    return pl.pallas_call(
        body,
        out_shape=shape(1, rows * len(blocks), width),
        in_specs=[vmem() for _ in blocks],
        out_specs=vmem(),
        compiler_params=params(),
        cost_estimate=cost(0, 64 << 10),
    )(*blocks)


def expert_math(pieces, ready, me, w_gate, turned, w_up, w_down, experts, splits):
    blocks = sum(splits)
    width, hid = w_gate.shape
    _, rows, full = pieces[0].shape
    half = rows // 2
    m = blocks * half
    count, had = len(pieces), len(ready)

    def body(*refs):
        early, refs = refs[count : count + had], refs[:count] + refs[count + had :]
        me_ref, wg_ref, gw_ref, dw_ref, wu_ref, wd_ref = refs[count : count + 6]
        outs = refs[count + 6 :]
        parts, (t_ref, do_ref, h_ref, dg_ref, du_ref) = outs[: len(splits)], outs[len(splits) :]
        x = jnp.concatenate([r[...] for r in refs[:count]], axis=0)
        token, coef, dout = rows_of(x, width, me_ref[0], experts)
        if had:
            token = jnp.concatenate([early[0][...], token], axis=0)
            coef = jnp.concatenate([early[1][:, :1], coef], axis=0)
            dout = jnp.concatenate([early[2][...], dout], axis=0)
        t_ref[...], do_ref[...] = token, dout
        gate = dot(token, wg_ref[...])
        sig = jax.nn.sigmoid(gate)
        swish = gate * sig
        upper = dot(token, wu_ref[...])
        dact = dot(dout, dw_ref[...])
        hidden = (swish * upper).astype(BF16)
        dgate = (dact * upper * sig * (1.0 + gate * (1.0 - sig))).astype(BF16)
        dupper = (dact * swish).astype(BF16)
        h_ref[...], dg_ref[...], du_ref[...] = hidden, dgate, dupper
        part = (coef * dot(hidden, wd_ref[...])).astype(BF16).reshape(blocks, half, width)
        mid = width // 2
        back = [dot(wu_ref[:mid], dupper, 1, 1).T, dot(dupper, wu_ref[mid:], 1, 1)]
        back = dot(dgate, gw_ref[...]) + jnp.concatenate(back, axis=1)
        back = back.astype(BF16).reshape(blocks, half, width)
        at = 0
        for ref, n in zip(parts, splits):
            ref[:, :half] = part[at : at + n]
            ref[:, half:] = back[at : at + n]
            at += n

    outs = [shape(n, rows, width) for n in splits]
    outs += [shape(m, width), shape(m, width), shape(m, hid), shape(m, hid), shape(m, hid)]
    got = pl.pallas_call(
        body,
        out_shape=outs,
        in_specs=[vmem()] * (count + had) + [pl.BlockSpec(memory_space=pltpu.SMEM)] + [vmem()] * 5,
        out_specs=[vmem() for _ in outs],
        compiler_params=params(LARGE),
        cost_estimate=cost(12 * m * width * hid, 10 << 20),
    )(*pieces, *ready, me, w_gate, *turned, w_up, w_down)
    return list(got[: len(splits)]), got[len(splits) :]


def weight_grads(left, rights, steps):
    m, rows = left.shape
    cols = rights[0].shape[1]
    steps = steps if rows % (128 * steps) == 0 else 1
    tile = rows // steps

    def body(l_ref, *refs):
        for r_ref, o_ref in zip(refs[: len(rights)], refs[len(rights) :]):
            o_ref[...] = dot(l_ref[...], r_ref[...], 0, 0).astype(BF16)

    return pl.pallas_call(
        body,
        grid=(steps,),
        out_shape=[shape(rows, cols) for _ in rights],
        in_specs=[pl.BlockSpec((m, tile), lambda i: (0, i))] + [pl.BlockSpec((m, cols), lambda i: (0, 0)) for _ in rights],
        out_specs=[pl.BlockSpec((tile, cols), lambda i: (i, 0)) for _ in rights],
        compiler_params=params(LARGE),
        cost_estimate=cost(2 * m * rows * cols * len(rights), 2 * rows * cols * len(rights)),
    )(left, *rights)


def add(terms, splits):
    outs = [shape(n, *terms[0].shape[1:], dtype=BF16 if i else F32) for i, n in enumerate(splits)]

    def body(*refs):
        total = sum(r[...].astype(F32) for r in refs[: len(terms)])
        at = 0
        for ref, n in zip(refs[len(terms) :], splits):
            ref[...] = total[at : at + n].astype(ref.dtype)
            at += n

    return pl.pallas_call(
        body,
        out_shape=outs,
        in_specs=[vmem() for _ in terms],
        out_specs=[vmem() for _ in outs],
        compiler_params=params(),
        cost_estimate=cost(0, 64 << 10),
    )(*terms)


def add_ungroup(terms, after):
    _, rows, width = terms[0].shape
    outs = [shape(1, 2 * ROWS, width, dtype=BF16 if i else F32) for i in range(GROUP)]

    def body(*refs):
        total = sum(r[...].astype(F32) for r in refs[: len(terms)])[0]
        low = lax.broadcasted_iota(jnp.int32, (2 * ROWS, 1), 0) < ROWS
        for i, ref in enumerate(refs[-GROUP:]):
            at = i // 2 * 2 * ROWS
            out, back = total[at : at + 2 * ROWS], total[rows // 2 + at : rows // 2 + at + 2 * ROWS]
            if i % 2:
                block = jnp.where(low, pltpu.roll(out, ROWS, 0), back)
            else:
                block = jnp.where(low, out, pltpu.roll(back, ROWS, 0))
            ref[0] = block.astype(ref.dtype)

    return pl.pallas_call(
        body,
        out_shape=outs,
        in_specs=[vmem() for _ in terms] + [hbm() for _ in after],
        out_specs=[vmem() for _ in outs],
        compiler_params=params(),
        cost_estimate=cost(0, 64 << 10),
    )(*terms, *outside(after))


def add_pair(one, two):
    def body(a_ref, b_ref, o_ref):
        o_ref[...] = (a_ref[...].astype(F32) + b_ref[...].astype(F32)).astype(BF16)

    return pl.pallas_call(
        body,
        out_shape=shape(*one.shape),
        in_specs=[vmem(), vmem()],
        out_specs=vmem(),
        compiler_params=params(),
        cost_estimate=cost(0, 64 << 10),
    )(one, two)


def finish(terms, after=()):
    _, _, width = terms[0].shape

    def body(*refs):
        total = refs[0][...].astype(F32)
        for r in refs[1 : len(terms)]:
            total += r[...].astype(F32)
        out_ref, back_ref = refs[len(terms) + len(after) :]
        out_ref[...] = total[0, :ROWS].astype(BF16)
        back_ref[...] = total[0, ROWS:].astype(BF16)

    return pl.pallas_call(
        body,
        out_shape=[shape(ROWS, width)] * 2,
        in_specs=[vmem() for _ in terms] + [hbm() for _ in after],
        out_specs=[vmem(), vmem()],
        compiler_params=params(),
        cost_estimate=cost(0, 64 << 10),
    )(*terms, *outside(after))


def on_device(tokens, route_ids, route_weights, w_gate, w_up, w_down, grad_out):
    experts = w_gate.shape[0] * lax.axis_size("expert")
    core = lax.axis_size("dp")
    total = lax.axis_size("expert") * core
    plan = stages(total, core)
    me = lax.axis_index("expert").astype(jnp.int32).reshape(1)
    wg, wu, wd = w_gate[0], w_up[0], w_down[0]

    block = pack(tokens, route_ids, route_weights, grad_out, experts)
    block = regroup([block] + exchange_all(block, plan[0], total))
    for masks in plan[1:]:
        held = [block] + exchange_all(block, masks, total)
        block = jnp.concatenate(held, axis=0)
    wg, own = fetch(wg, held[0])
    wd, wu, *turned = fetch_behind((wd, wu), wg, held, me, experts)
    turned, ready = turned[:2], turned[2:]
    pieces = held + [exchange(h, core, total) for h in [own] + held[1:]]

    ways = len(held)
    groups = total // GROUP
    size = groups // 2 // ways
    if groups <= CHUNK:
        parts, kept = expert_math(pieces[len(held) :], ready, me, wg, turned, wu, wd, experts, [size] * (2 * ways))
    else:
        whole = jnp.concatenate(pieces, axis=0)
        sums, saved = [], []
        for at in range(0, groups, CHUNK):
            (got,), rest = expert_math([whole[at : at + CHUNK]], [], me, wg, turned, wu, wd, experts, [CHUNK])
            sums.append(got)
            saved.append(rest)
        got = jnp.concatenate(sums, axis=0)
        parts = [got[at : at + size] for at in range(0, groups, size)]
        kept = [jnp.concatenate(p, axis=0) for p in zip(*saved)]
    token, dout, hidden, dgate, dupper = kept

    gate_grad, up_grad = weight_grads(token, [dgate, dupper], 2)
    (down_grad,) = weight_grads(hidden, [dout], 2)

    keep, send = parts[:ways], parts[ways:]
    arrived = [exchange(p, core, total) for p in send[::-1]][::-1]
    sums = [add_pair(keep[at], arrived[at]) for at in range(1, ways)]
    terms = [*exchange_all(sums[::-1], plan[-1][::-1], total), keep[0], arrived[0]]
    for masks in reversed(plan[1:-1]):
        ways = len(masks) + 1
        mine, *others = add(terms, [terms[0].shape[0] // ways] * ways)
        terms = [mine, *exchange_all(others[::-1], masks[::-1], total)]
    mine, *others = add_ungroup(terms, (gate_grad,))
    terms = [mine, *exchange_all(others[::-1], plan[0][::-1], total)]
    mixed, back = finish(terms, (down_grad,))
    return mixed, back, gate_grad[None], up_grad[None], down_grad[None]


def solution(mesh):
    rows = P(("groups", "expert", "dp"), None)
    in_specs = (rows, rows, rows, P("expert", None, "dp"), P("expert", None, "dp"), P("expert", "dp", None), rows)
    hidden = P(("groups", "expert"), None, "dp")
    out_specs = (rows, rows, hidden, hidden, P(("groups", "expert"), "dp", None))
    return jax.shard_map(on_device, mesh=mesh, in_specs=in_specs, out_specs=out_specs, check_vma=False)
```
